768 devices in a mesh: dp: 8 (over y), pack: 12 (over z), mp: 8 (over x, core).
Axes of the slice: x: 4, y: 8, z: 12, core: 2. Of those that a mesh axis runs over, the one named last changes fastest.
Arguments:
- tile_activity: bfloat16 [384, 256, 1536], P(('dp', 'pack'), None, 'mp'), may hold values from -100 to 100
- tokens_per_picture: int32 [384, 4], P(('dp', 'pack')), may hold values from 16 to 128, as said below
- slot_destinations: int32 [384], P(('dp', 'pack')), may hold values from -1 to 23, as said below
- caption_indices: int32 [384, 4], P(('dp', 'pack')), may hold values from 0 to 767, as said below
- attention_projections: bfloat16 [3, 1536, 1536], P(None, None, 'mp'), may hold values from -1 to 1
- caption_vectors: bfloat16 [768, 1536], P(('dp', 'pack'), 'mp'), may hold values from -600 to 600
- score_inverse_heat: float32 [1], replicated, may hold values from 4 to 12
- score_shift: float32 [1], replicated, may hold values from -3 to 0
Outputs:
- image_grads: float32 [768, 1536], P(('dp', 'pack'), 'mp')
- text_grads: float32 [768, 1536], P(('dp', 'pack'), 'mp')
The draws below stay inside these ranges and needn't reach their ends.
Inputs may be any that keep to these rules, and one draw needn't show every extreme that they name: `slot_destinations`: within one dp index, the block slots of the 12 pack devices name every value 0 .. 23 exactly once; -1 marks an empty slot. No device sends more than 1 block to one destination, and in every dp index some device holds 4 real blocks. `caption_indices`: over the images of non-empty block slots every text index appears exactly once. `tokens_per_picture`: in every block slot the 4 counts sum to 256; exactly one of them is 128 and each other is at least 16.
All inputs are finite; a program needn't handle non-finite values.
Results may differ from the reference program's by a relative error of at most 0.0045.
Values may be sent and summed in bfloat16 or wider, within the bound.
A program may use at most 32 MiB of HBM per device.

```python
import math
import jax
import jax.numpy as jnp
from jax import lax

D = 1536
HEADS = 24
HEAD = 64
BLK = 256
IPB = 4
DEST = 2
SRC = 4
SRC_BLOCKS = 384
DEST_BLOCKS = 192
IMAGES = 768
TEXTS = 768
N_DP = 8
N_PACK = 12


def route_table(key):
    group_keys = jax.random.split(key, N_DP)

    def group_table(group_key):
        key_full, key_extra, key_slots, key_label = jax.random.split(group_key, 4)
        full_device = jax.random.randint(key_full, (), 0, N_PACK)
        extra_total = N_PACK * DEST - SRC - (N_PACK - 1)
        shuffled = jax.random.permutation(key_extra, (N_PACK - 1) * (SRC - 1))
        extras = jnp.sum((shuffled < extra_total).reshape(N_PACK - 1, SRC - 1).astype(jnp.int32), axis=1)
        device_ids = jnp.arange(N_PACK, dtype=jnp.int32)
        shifted = jnp.clip(device_ids - (device_ids > full_device).astype(jnp.int32), 0, N_PACK - 2)
        real_counts = jnp.where(device_ids == full_device, SRC, 1 + extras[shifted])

        def slot_order(slot_key):
            return jax.random.permutation(slot_key, SRC)
        slot_ranks = jax.vmap(slot_order)(jax.random.split(key_slots, N_PACK))
        occupied = (slot_ranks < real_counts[:, None]).reshape(-1).astype(jnp.int32)
        running = jnp.cumsum(occupied) - occupied
        relabel = jax.random.permutation(key_label, N_PACK)
        return jnp.where(occupied > 0, relabel[running % N_PACK] * DEST + running // N_PACK, -1).astype(jnp.int32)
    return jax.vmap(group_table)(group_keys).reshape(SRC_BLOCKS)


def draw_slot_destinations(key, part):
    table = route_table(key)
    return table.astype(jnp.int32)


def draw_tokens_per_picture(key, part):
    key = jax.random.fold_in(key, 13)
    key_cuts, key_order = jax.random.split(key, 2)
    smallest = BLK // 16
    spare = BLK - BLK // 2 - (IPB - 1) * smallest
    cuts = jnp.sort(jax.random.randint(key_cuts, (SRC_BLOCKS, IPB - 2), 0, spare + 1), axis=1)
    edges = jnp.concatenate([jnp.zeros((SRC_BLOCKS, 1), jnp.int32), cuts.astype(jnp.int32), jnp.full((SRC_BLOCKS, 1), spare, jnp.int32)], axis=1)
    others = edges[:, 1:] - edges[:, :-1] + smallest
    row = jnp.concatenate([jnp.full((SRC_BLOCKS, 1), BLK // 2, jnp.int32), others], axis=1)

    def order_one(order_key):
        return jax.random.permutation(order_key, IPB)
    orders = jax.vmap(order_one)(jax.random.split(key_order, SRC_BLOCKS))
    return jnp.take_along_axis(row, orders, axis=1).astype(jnp.int32)


def draw_caption_indices(key, part):
    table = route_table(key)
    key = jax.random.fold_in(key, 3)
    key_perm, key_fill = jax.random.split(key, 2)
    real_images = jnp.repeat((table >= 0).astype(jnp.int32), IPB)
    running = jnp.cumsum(real_images) - real_images
    text_order = jax.random.permutation(key_perm, TEXTS).astype(jnp.int32)
    spare = jax.random.randint(key_fill, (SRC_BLOCKS * IPB,), 0, TEXTS)
    chosen = jnp.where(real_images > 0, text_order[jnp.clip(running, 0, TEXTS - 1)], spare)
    return chosen.reshape(SRC_BLOCKS, IPB).astype(jnp.int32)


def draw_tile_activity(key, part):
    key = jax.random.fold_in(key, 5)
    key_noise, key_cols = jax.random.split(key, 2)
    noise = jnp.clip(jax.random.normal(key_noise, (SRC_BLOCKS, BLK, D), jnp.float32), -6.0, 6.0)
    column_scale = jnp.exp(jax.random.uniform(key_cols, (D,), jnp.float32, math.log(0.5), math.log(2.0)))
    return (noise * column_scale).astype(jnp.bfloat16)


def draw_attention_projections(key, part):
    key = jax.random.fold_in(key, 7)
    weights = jnp.clip(jax.random.normal(key, (3, D, D), jnp.float32), -4.0, 4.0) * (1.0 / math.sqrt(D))
    return weights.astype(jnp.bfloat16)


def draw_caption_vectors(key, part):
    key = jax.random.fold_in(key, 11)
    key_noise, key_rows, key_cols = jax.random.split(key, 3)
    noise = jnp.clip(jax.random.normal(key_noise, (TEXTS, D), jnp.float32), -6.0, 6.0)
    row_scale = jnp.exp(jax.random.uniform(key_rows, (TEXTS, 1), jnp.float32, 0.0, math.log(10.0)))
    column_scale = jnp.exp(jax.random.uniform(key_cols, (D,), jnp.float32, 0.0, math.log(10.0)))
    return (noise * row_scale * column_scale).astype(jnp.bfloat16)


def setup_inputs(seed: int = 0) -> dict:
    arg_keys = jax.random.split(jax.random.key(seed), 9)
    tile_activity = draw_tile_activity(jax.random.fold_in(arg_keys[8], 71), 0)
    tokens_per_picture = draw_tokens_per_picture(jax.random.fold_in(arg_keys[8], 71), 0)
    slot_destinations = draw_slot_destinations(jax.random.fold_in(arg_keys[8], 71), 0)
    caption_indices = draw_caption_indices(jax.random.fold_in(arg_keys[8], 71), 0)
    attention_projections = draw_attention_projections(jax.random.fold_in(arg_keys[8], 71), 0)
    caption_vectors = draw_caption_vectors(jax.random.fold_in(arg_keys[8], 71), 0)
    score_inverse_heat = jnp.clip(jax.random.uniform(arg_keys[6], (1,), jnp.float32, 4.0, 12.0), 4.0, 12.0)
    score_shift = jnp.clip(jax.random.uniform(arg_keys[7], (1,), jnp.float32, -3.0, 0.0), -3.0, 0.0)
    return dict(tile_activity=tile_activity, tokens_per_picture=tokens_per_picture, slot_destinations=slot_destinations, caption_indices=caption_indices, attention_projections=attention_projections, caption_vectors=caption_vectors, score_inverse_heat=score_inverse_heat, score_shift=score_shift)


def reference(tile_activity, tokens_per_picture, slot_destinations, caption_indices, attention_projections, caption_vectors, score_inverse_heat, score_shift):
    global_group = (jnp.arange(SRC_BLOCKS, dtype=jnp.int32) // (N_PACK * SRC)).astype(jnp.int32)
    target = jnp.where(slot_destinations >= 0, global_group * (N_PACK * DEST) + slot_destinations, DEST_BLOCKS).astype(jnp.int32)
    routed = jnp.zeros((DEST_BLOCKS, BLK, D), jnp.bfloat16).at[target].set(tile_activity, mode='drop')
    image_sizes = jnp.ones((DEST_BLOCKS, IPB), jnp.int32).at[target].set(tokens_per_picture, mode='drop')
    pair_ids = jnp.zeros((DEST_BLOCKS, IPB), jnp.int32).at[target].set(caption_indices, mode='drop')

    def attend(item):
        rows, sizes_here = item
        projected = []
        for which in range(3):
            full = jnp.dot(rows, attention_projections[which], preferred_element_type=jnp.float32).astype(jnp.bfloat16)
            projected.append(lax.optimization_barrier(full).astype(jnp.float32).reshape(BLK, HEADS, HEAD))
        queries, key_rows, values = projected
        image_ends = jnp.cumsum(sizes_here)
        position = jnp.arange(BLK, dtype=jnp.int32)
        segment = lax.optimization_barrier(jnp.sum((position[None, :] >= image_ends[:, None]).astype(jnp.int32), axis=0))
        scores = jnp.einsum('phe,qhe->hpq', queries, key_rows) * HEAD ** (-0.5)
        same_image = segment[:, None] == segment[None, :]
        scores = jnp.where(same_image[None], scores, -1e+30)
        row_max = lax.optimization_barrier(jnp.max(scores, axis=-1, keepdims=True))
        exponent = jnp.exp(scores - row_max)
        probabilities = (exponent / lax.optimization_barrier(jnp.sum(exponent, axis=-1, keepdims=True))).astype(jnp.bfloat16)
        probabilities = lax.optimization_barrier(probabilities).astype(jnp.float32)
        attended = jnp.einsum('hpq,qhe->phe', probabilities, values)
        pooling = (segment[None, :] == jnp.arange(IPB, dtype=jnp.int32)[:, None]).astype(jnp.float32)
        pooling = pooling / sizes_here.astype(jnp.float32)[:, None]
        pooled = jnp.einsum('mp,phe->mhe', pooling, attended, precision=lax.Precision.HIGHEST)
        return pooled.reshape(IPB, D).astype(jnp.bfloat16)
    embeds = lax.map(attend, (routed, image_sizes)).reshape(IMAGES, D)
    pair_flat = pair_ids.reshape(IMAGES)
    smoothing_coefficient = score_inverse_heat[0]
    logit_offset_value = score_shift[0]
    similarity_products = jnp.dot(embeds, caption_vectors.T, preferred_element_type=jnp.float32)
    image_norm_factor = lax.rsqrt(lax.optimization_barrier(jnp.sum(embeds.astype(jnp.float32) ** 2, axis=1)) + 1e-06)
    text_norm_factor = lax.rsqrt(lax.optimization_barrier(jnp.sum(caption_vectors.astype(jnp.float32) ** 2, axis=1)) + 1e-06)
    pair_logit_matrix = smoothing_coefficient * similarity_products * image_norm_factor[:, None] * text_norm_factor[None, :] + logit_offset_value
    signed_pair_labels = jnp.where(pair_flat[:, None] == jnp.arange(TEXTS, dtype=jnp.int32)[None, :], 1.0, -1.0).astype(pair_logit_matrix.dtype)
    sigmoid_slopes = -signed_pair_labels * jax.nn.sigmoid(-signed_pair_labels * pair_logit_matrix) * smoothing_coefficient
    text_unit = caption_vectors.astype(jnp.float32) * text_norm_factor[:, None]
    image_unit = embeds.astype(jnp.float32) * image_norm_factor[:, None]
    image_grads = jnp.dot(sigmoid_slopes, text_unit, precision=lax.Precision.HIGHEST)
    text_grads = jnp.dot(sigmoid_slopes.T, image_unit, precision=lax.Precision.HIGHEST)
    return (image_grads, text_grads)
```

```python
import functools

import jax
import jax.numpy as jnp
from jax import lax
from jax.experimental import pallas as pl
from jax.experimental.pallas import tpu as pltpu
from jax.sharding import PartitionSpec as P

HEAD = 64
BLK = 256
IPB = 4
DEST = 2
SRC = 4
F32 = jnp.float32
BF16 = jnp.bfloat16
MESH = pl.DeviceIdType.MESH

LABEL_HI, LABEL_LO, PLACE, SQ0, SQ1, SQ2 = 192, 193, 194, 195, 196, 197


def dot(a, b):
    return jnp.dot(a, b, preferred_element_type=F32)


def dot_t(a, b):
    return lax.dot_general(a, b, (((1,), (1,)), ((), ())), preferred_element_type=F32)


def iota(shape, axis):
    return lax.broadcasted_iota(jnp.int32, shape, axis)


def split2(a):
    hi = a.astype(BF16)
    return hi, (a - hi.astype(F32)).astype(BF16)


def kernel(
    n_dp,
    n_pack,
    n_mp,
    tile_hbm,
    sizes_ref,
    dest_ref,
    caption_ref,
    proj_hbm,
    texts_ref,
    heat_ref,
    shift_ref,
    image_out,
    text_out,
    raw,
    proj,
    rows,
    w_main,
    w_low,
    w_high,
    qx,
    kx,
    pooled,
    text_rows,
    pack_rows,
    sims,
    own_text,
    own_image,
    text_terms,
    image_terms,
    load_sem,
    x_send,
    x_recv,
    t_send,
    t_recv,
    e_send,
    e_recv,
    s_send,
    s_recv,
    ty_send,
    ty_recv,
    iz_send,
    iz_recv,
):
    g, p, m = lax.axis_index("dp"), lax.axis_index("pack"), lax.axis_index("mp")
    chips = n_mp // 2
    chip, core = m // 2, m % 2
    right = ((chip + 1) % chips) * 2 + core
    left = ((chip + chips - 1) % chips) * 2 + core
    far = ((chip + 2) % chips) * 2 + core
    twin = chip * 2 + 1 - core
    width = texts_ref.shape[1]

    load_tile = pltpu.make_async_copy(tile_hbm, raw, load_sem.at[0])
    load_proj = pltpu.make_async_copy(proj_hbm, proj, load_sem.at[1])
    load_tile.start()
    load_proj.start()

    barrier = pltpu.get_barrier_semaphore()
    for d in range(1, n_mp):
        pl.semaphore_signal(barrier, inc=1, device_id={"mp": (m + d) % n_mp}, device_id_type=MESH)
    for d in range(1, n_dp):
        pl.semaphore_signal(barrier, inc=1, device_id={"dp": (g + d) % n_dp}, device_id_type=MESH)
    for d in range(1, n_pack):
        pl.semaphore_signal(
            barrier, inc=1, device_id={"pack": (p + d) % n_pack}, device_id_type=MESH
        )

    load_tile.wait()
    half = BLK // 2
    for s in range(SRC):
        rows[s, m, 0:BLK, :] = raw[s, :, 0:128]
        tail = jnp.concatenate(
            [raw[s, 0:half, 128:192].astype(F32), raw[s, half:BLK, 128:192].astype(F32)], axis=1
        )
        rows[s, m, BLK : BLK + half, :] = tail.astype(BF16)
    text_rows[g] = jnp.zeros((8, 256), F32)
    text_rows[g, :, 0:width] = texts_ref[...].astype(F32)

    pl.semaphore_wait(barrier, n_mp + n_dp + n_pack - 3)

    def remote(src, dst, send, recv, where):
        return pltpu.make_async_remote_copy(
            src_ref=src,
            dst_ref=dst,
            send_sem=send,
            recv_sem=recv,
            device_id=where,
            device_id_type=MESH,
        )

    mid = (BLK + half) // 2

    def own_to_right(s):
        return remote(rows.at[s, m], rows.at[s, m], x_send.at[s, 0], x_recv.at[s, 0], {"mp": right})

    def own_to_left(s):
        return remote(rows.at[s, m], rows.at[s, m], x_send.at[s, 1], x_recv.at[s, 1], {"mp": left})

    def own_to_twin(s):
        return remote(rows.at[s, m], rows.at[s, m], x_send.at[s, 2], x_recv.at[s, 2], {"mp": twin})

    def pass_right(s):
        part = rows.at[s, left, pl.ds(0, mid)]
        return remote(part, part, x_send.at[s, 3], x_recv.at[s, 3], {"mp": right})

    def pass_left(s):
        part = rows.at[s, right, pl.ds(mid, mid)]
        return remote(part, part, x_send.at[s, 4], x_recv.at[s, 4], {"mp": left})

    def share(s, whose, k):
        part = rows.at[s, whose]
        return remote(part, part, x_send.at[s, k], x_recv.at[s, k], {"mp": twin})

    def got(s, k, part):
        return remote(part, part, x_send.at[s, k], x_recv.at[s, k], {"mp": twin})

    for s in range(SRC):
        own_to_right(s).start()
        own_to_left(s).start()
        own_to_twin(s).start()

    def text_copy(d):
        return remote(
            text_rows.at[g], text_rows.at[g], t_send.at[d], t_recv.at[g], {"dp": (g + d) % n_dp}
        )

    for d in range(1, n_dp):
        text_copy(d).start()

    load_proj.wait()
    w_low[...] = jnp.zeros_like(w_low)
    w_high[...] = jnp.zeros_like(w_high)
    for c in range(3):
        for k in range(n_mp):
            w_main[c, k * 128 : k * 128 + 128, :] = proj[c, k * width : k * width + 128, :]
            rest = proj[c, k * width + 128 : k * width + 192, :]
            w_low[c, k * 128 : k * 128 + 64, :] = rest
            w_high[c, k * 128 + 64 : k * 128 + 128, :] = rest
    pooled[...] = jnp.zeros_like(pooled)

    def pass_on(s):
        got(s, 0, rows.at[s, left]).wait_recv()
        pass_right(s).start()
        share(s, left, 5).start()
        got(s, 1, rows.at[s, right]).wait_recv()
        pass_left(s).start()
        share(s, right, 6).start()

    lane = iota((BLK, 256), 1)

    def attend(s):
        e1 = sizes_ref[s, 0]
        e2 = e1 + sizes_ref[s, 1]
        e3 = e2 + sizes_ref[s, 2]

        def image_of(position):
            return (
                (position >= e1).astype(jnp.int32)
                + (position >= e2).astype(jnp.int32)
                + (position >= e3).astype(jnp.int32)
            )

        same = image_of(iota((BLK, 256), 0)) == lane - width
        extra = (lane >= width) & (lane < width + IPB)
        qx[...] = jnp.where(extra & same, -1e30, 0.0).astype(BF16)
        kx[...] = jnp.where(extra & jnp.logical_not(same), 1.0, 0.0).astype(BF16)

        main = jnp.concatenate([rows[s, k, 0:BLK, :] for k in range(n_mp)], axis=1)
        tails = jnp.concatenate([rows[s, k, BLK : BLK + half, :] for k in range(n_mp)], axis=1)

        def project(c):
            return dot(main, w_main[c]) + jnp.concatenate(
                [dot(tails, w_low[c]), dot(tails, w_high[c])], axis=0
            )

        qx[:, 0:width] = (project(0) * HEAD**-0.5).astype(BF16)
        kx[:, 0:width] = project(1).astype(BF16)
        values = project(2).astype(BF16)
        keys = kx[...]
        queries = qx[...]

        row16 = iota((SRC * IPB, BLK), 0)
        member = (row16 // IPB == s) & (row16 % IPB == image_of(iota((SRC * IPB, BLK), 1)))
        member = jnp.where(member, 1.0, 0.0).astype(BF16)
        weights = []
        for h in range(width // HEAD):
            keep = ((lane >= h * HEAD) & (lane < (h + 1) * HEAD)) | (lane >= width)
            scores = dot_t(keys, jnp.where(keep, queries, jnp.zeros_like(queries)))
            exponent = jnp.exp(scores - jnp.max(scores, axis=0, keepdims=True))
            inverse = 1.0 / jnp.sum(exponent, axis=0, keepdims=True)
            weights.append(dot_t(member, (exponent * inverse).astype(BF16)))
        hi, lo = split2(jnp.concatenate(weights, axis=0))
        sums = dot(hi, values) + dot(lo, values)
        col = iota((SRC * IPB, width), 1)
        picked = sums[0 : SRC * IPB]
        for h in range(1, width // HEAD):
            picked = jnp.where(
                col >= h * HEAD, sums[h * SRC * IPB : (h + 1) * SRC * IPB], picked
            )
        pooled[...] += picked

    pass_on(0)

    def slot(s, carry):
        @pl.when(s + 1 < SRC)
        def _():
            pass_on(s + 1)

        got(s, 3, rows.at[s, far, pl.ds(0, mid)]).wait_recv()
        got(s, 4, rows.at[s, far, pl.ds(mid, mid)]).wait_recv()
        share(s, far, 7).start()
        for k, offset in ((2, chip), (5, left // 2), (6, right // 2), (7, far // 2)):
            got(s, k, rows.at[s, offset * 2 + 1 - core]).wait_recv()
        attend(s)
        return carry

    lax.fori_loop(0, SRC, slot, 0)

    r = iota((SRC * IPB, 1), 0)
    label = jnp.zeros((SRC * IPB, 1), jnp.int32)
    place = jnp.zeros((SRC * IPB, 1), jnp.int32)
    count = jnp.ones((SRC * IPB, 1), jnp.int32)
    for s in range(SRC):
        for n in range(IPB):
            here = r == s * IPB + n
            label = jnp.where(here, caption_ref[s, n], label)
            place = jnp.where(here, dest_ref[s] * IPB + n, place)
            count = jnp.where(here, sizes_ref[s, n], count)
    embeds = (pooled[...] * (1.0 / count.astype(F32))).astype(BF16)
    squares = jnp.sum(embeds.astype(F32) * embeds.astype(F32), axis=1, keepdims=True)
    sq0 = squares.astype(BF16).astype(F32)
    sq1 = (squares - sq0).astype(BF16).astype(F32)
    sq2 = squares - sq0 - sq1
    col = iota((SRC * IPB, 256), 1)
    extended = jnp.zeros((SRC * IPB, 256), F32)
    for at, value in (
        (LABEL_HI, (label // 8).astype(F32)),
        (LABEL_LO, (label % 8).astype(F32)),
        (PLACE, place.astype(F32)),
        (SQ0, sq0),
        (SQ1, sq1),
        (SQ2, sq2),
    ):
        extended = jnp.where(col == at, value, extended)
    pack_rows[p] = extended.astype(BF16)
    pack_rows[p, :, 0:width] = embeds

    def embed_copy(d):
        return remote(
            pack_rows.at[p], pack_rows.at[p], e_send.at[d], e_recv.at[p], {"pack": (p + d) % n_pack}
        )

    for d in range(1, n_pack):
        embed_copy(d).start()

    for d in range(1, n_dp):
        src = (g + d) % n_dp
        remote(
            text_rows.at[src], text_rows.at[src], t_send.at[d], t_recv.at[src], {"dp": src}
        ).wait_recv()
    n_texts = n_dp * text_rows.shape[1]
    text_all = text_rows[...].reshape(n_texts, 256)
    text_all = jnp.where(iota((n_texts, 256), 1) < width, text_all, 0.0)
    text_squares = jnp.sum(text_all * text_all, axis=1, keepdims=True)
    text_bf = text_all.astype(BF16)
    pick = iota((16, 256), 1)
    is_square = (pick >= SQ0) & (pick <= SQ2)
    low = iota((16, 256), 0) < 8
    reads = jnp.where(low & is_square, 1.0, 0.0)
    reads = jnp.where(jnp.logical_not(low) & (pick == LABEL_HI), 8.0, reads)
    reads = jnp.where(jnp.logical_not(low) & (pick == LABEL_LO), 1.0, reads)
    left_side = jnp.concatenate([text_bf, reads.astype(BF16)], axis=0)

    for d in range(1, n_pack):
        src = (p + d) % n_pack
        remote(
            pack_rows.at[src], pack_rows.at[src], e_send.at[d], e_recv.at[src], {"pack": src}
        ).wait_recv()

    n_slots = n_pack * SRC * IPB
    n_images = n_pack * DEST * IPB
    loose = pack_rows[...].reshape(n_slots, 256)
    find = jnp.where(iota((128, 256), 1) == PLACE, 1.0, 0.0).astype(BF16)
    placing = dot_t(find, loose) == iota((128, n_slots), 0).astype(F32)
    packed = dot(jnp.where(placing, 1.0, 0.0).astype(BF16), loose).astype(BF16)

    products = dot_t(left_side, packed)
    image_lane = iota((n_texts, 128), 1)
    sims[m, 0:n_texts, :] = jnp.where(image_lane < n_images, products[0:n_texts], text_squares)
    sims[m, n_texts : n_texts + 8, :] = products[n_texts : n_texts + 8]
    labels = products[n_texts + 8 : n_texts + 9]

    def sims_copy(d):
        return remote(sims.at[m], sims.at[m], s_send.at[d], s_recv.at[m], {"mp": (m + d) % n_mp})

    for d in range(1, n_mp):
        sims_copy(d).start()
    text_row = iota((n_texts, 128), 0)
    matching = labels == (((text_row // 8) * n_pack + p) * 8 + text_row % 8).astype(F32)
    sign = jnp.where(matching, 1.0, -1.0)
    for d in range(1, n_mp):
        src = (m + d) % n_mp
        remote(sims.at[src], sims.at[src], s_send.at[d], s_recv.at[src], {"mp": src}).wait_recv()
    total = sims[0]
    for k in range(1, n_mp):
        total = total + sims[k]
    cosine = total[0:n_texts]
    image_scale = lax.rsqrt(total[n_texts : n_texts + 1] + 1e-06)
    text_scale = lax.rsqrt(
        jnp.sum(jnp.where(image_lane == n_images, cosine, 0.0), axis=1, keepdims=True) + 1e-06
    )
    heat = heat_ref[0]
    logits = heat * cosine * image_scale * text_scale + shift_ref[0]
    slopes = -sign * jax.nn.sigmoid(-sign * logits) * heat
    slopes = jnp.where(image_lane < n_images, slopes, 0.0)

    hi, lo = split2(slopes * text_scale)
    contract0 = (((0,), (0,)), ((), ()))
    image_part = lax.dot_general(hi, text_bf, contract0, preferred_element_type=F32)
    image_part += lax.dot_general(lo, text_bf, contract0, preferred_element_type=F32)
    own_image[...] = image_part[0:n_images].reshape(n_pack, 8, 256)

    def image_copy(d):
        to = (p + d) % n_pack
        return remote(
            own_image.at[to], image_terms.at[p], iz_send.at[d], iz_recv.at[p], {"pack": to}
        )

    for d in range(1, n_pack):
        image_copy(d).start()

    hi, lo = split2(slopes * jnp.where(iota((1, 128), 1) < n_images, image_scale, 0.0))
    text_part = dot(hi, packed) + dot(lo, packed)
    own_text[...] = text_part.reshape(n_dp, 8, 256)

    def text_term_copy(d):
        to = (g + d) % n_dp
        return remote(own_text.at[to], text_terms.at[g], ty_send.at[d], ty_recv.at[g], {"dp": to})

    for d in range(1, n_dp):
        text_term_copy(d).start()

    image_terms[p] = own_image[p]
    text_terms[g] = own_text[g]
    for d in range(1, n_dp):
        src = (g + d) % n_dp
        remote(
            own_text.at[src], text_terms.at[src], ty_send.at[d], ty_recv.at[src], {"dp": src}
        ).wait_recv()
    text_out[...] = jnp.sum(text_terms[...], axis=0)[:, 0:width]
    for d in range(1, n_pack):
        src = (p + d) % n_pack
        remote(
            own_image.at[src], image_terms.at[src], iz_send.at[d], iz_recv.at[src], {"pack": src}
        ).wait_recv()
    image_out[...] = jnp.sum(image_terms[...], axis=0)[:, 0:width]

    def sent(s, carry):
        own_to_right(s).wait_send()
        own_to_left(s).wait_send()
        own_to_twin(s).wait_send()
        pass_right(s).wait_send()
        pass_left(s).wait_send()
        share(s, left, 5).wait_send()
        share(s, right, 6).wait_send()
        share(s, far, 7).wait_send()
        return carry

    lax.fori_loop(0, SRC, sent, 0)
    for d in range(1, n_dp):
        text_copy(d).wait_send()
        text_term_copy(d).wait_send()
    for d in range(1, n_pack):
        embed_copy(d).wait_send()
        image_copy(d).wait_send()
    for d in range(1, n_mp):
        sims_copy(d).wait_send()


def on_device(
    n_dp,
    n_pack,
    n_mp,
    tile_activity,
    tokens_per_picture,
    slot_destinations,
    caption_indices,
    attention_projections,
    caption_vectors,
    score_inverse_heat,
    score_shift,
):
    width = caption_vectors.shape[1]
    depth = attention_projections.shape[1]
    n_texts = n_dp * caption_vectors.shape[0]
    vmem = pl.BlockSpec(memory_space=pltpu.VMEM)
    smem = pl.BlockSpec(memory_space=pltpu.SMEM)
    hbm = pl.BlockSpec(memory_space=pl.ANY)
    dma = pltpu.SemaphoreType.DMA
    return pl.pallas_call(
        functools.partial(kernel, n_dp, n_pack, n_mp),
        out_shape=(
            jax.ShapeDtypeStruct(caption_vectors.shape, F32),
            jax.ShapeDtypeStruct(caption_vectors.shape, F32),
        ),
        in_specs=[hbm, smem, smem, smem, hbm, vmem, smem, smem],
        out_specs=(vmem, vmem),
        scratch_shapes=[
            pltpu.VMEM((SRC, BLK, width), BF16),
            pltpu.VMEM((3, depth, width), BF16),
            pltpu.VMEM((SRC, n_mp, BLK + BLK // 2, 128), BF16),
            pltpu.VMEM((3, n_mp * 128, width), BF16),
            pltpu.VMEM((3, n_mp * 128, width), BF16),
            pltpu.VMEM((3, n_mp * 128, width), BF16),
            pltpu.VMEM((BLK, 256), BF16),
            pltpu.VMEM((BLK, 256), BF16),
            pltpu.VMEM((SRC * IPB, width), F32),
            pltpu.VMEM((n_dp, 8, 256), F32),
            pltpu.VMEM((n_pack, SRC * IPB, 256), BF16),
            pltpu.VMEM((n_mp, n_texts + 8, 128), F32),
            pltpu.VMEM((n_dp, 8, 256), F32),
            pltpu.VMEM((n_pack, 8, 256), F32),
            pltpu.VMEM((n_dp, 8, 256), F32),
            pltpu.VMEM((n_pack, 8, 256), F32),
            dma((2,)),
            dma((SRC, 8)),
            dma((SRC, 8)),
            dma((n_dp,)),
            dma((n_dp,)),
            dma((n_pack,)),
            dma((n_pack,)),
            dma((n_mp,)),
            dma((n_mp,)),
            dma((n_dp,)),
            dma((n_dp,)),
            dma((n_pack,)),
            dma((n_pack,)),
        ],
        compiler_params=pltpu.CompilerParams(
            collective_id=0, has_side_effects=True, vmem_limit_bytes=40 * 1024 * 1024
        ),
        name="contrastive_step",
    )(
        tile_activity,
        tokens_per_picture,
        slot_destinations,
        caption_indices,
        attention_projections,
        caption_vectors,
        score_inverse_heat,
        score_shift,
    )


def solution(mesh):
    sizes = (mesh.shape["dp"], mesh.shape["pack"], mesh.shape["mp"])
    return jax.shard_map(
        functools.partial(on_device, *sizes),
        mesh=mesh,
        in_specs=(
            P(("dp", "pack"), None, "mp"),
            P(("dp", "pack"), None),
            P(("dp", "pack")),
            P(("dp", "pack"), None),
            P(None, None, "mp"),
            P(("dp", "pack"), "mp"),
            P(),
            P(),
        ),
        out_specs=(P(("dp", "pack"), "mp"), P(("dp", "pack"), "mp")),
        check_vma=False,
    )
```

```python
import functools

import jax
import jax.numpy as jnp
from jax import lax
from jax.experimental import pallas as pl
from jax.experimental.pallas import tpu as pltpu
from jax.sharding import PartitionSpec as P

HEAD = 64
BLK = 256
IPB = 4
DEST = 2
SRC = 4
F32 = jnp.float32
BF16 = jnp.bfloat16
MESH = pl.DeviceIdType.MESH

LABEL_HI, LABEL_LO, PLACE, SQ0, SQ1, SQ2 = 192, 193, 194, 195, 196, 197


def dot(a, b):
    return jnp.dot(a, b, preferred_element_type=F32)


def dot_t(a, b):
    return lax.dot_general(a, b, (((1,), (1,)), ((), ())), preferred_element_type=F32)


def iota(shape, axis):
    return lax.broadcasted_iota(jnp.int32, shape, axis)


def split2(a):
    hi = a.astype(BF16)
    return hi, (a - hi.astype(F32)).astype(BF16)


def far_first(n):
    return sorted(range(1, n), key=lambda d: -min(d, n - d))


def kernel(
    n_dp,
    n_pack,
    n_mp,
    tile_hbm,
    info_hbm,
    proj_hbm,
    texts_ref,
    heat_hbm,
    shift_hbm,
    image_out,
    text_out,
    info_ref,
    heat_ref,
    shift_ref,
    proj,
    rows,
    pooled,
    text_rows,
    pack_rows,
    sims,
    halves,
    own_text,
    own_image,
    text_terms,
    image_terms,
    load_sem,
    x_send,
    x_recv,
    t_send,
    t_recv,
    e_send,
    e_recv,
    s_send,
    s_recv,
    ty_send,
    ty_recv,
    iz_send,
    iz_recv,
):
    g, p, m = lax.axis_index("dp"), lax.axis_index("pack"), lax.axis_index("mp")
    chips = n_mp // 2
    chip, core = m // 2, m % 2
    right = ((chip + 1) % chips) * 2 + core
    left = ((chip + chips - 1) % chips) * 2 + core
    far = ((chip + 2) % chips) * 2 + core
    twin = chip * 2 + 1 - core
    width = texts_ref.shape[1]

    load_tile = pltpu.make_async_copy(tile_hbm, rows.at[:, m], load_sem.at[0])
    load_proj = pltpu.make_async_copy(proj_hbm, proj, load_sem.at[1])
    load_tile.start()
    load_proj.start()
    scalars = [
        pltpu.make_async_copy(src, dst, load_sem.at[2 + i])
        for i, (src, dst) in enumerate(
            (
                (info_hbm, info_ref),
                (heat_hbm, heat_ref),
                (shift_hbm, shift_ref),
            )
        )
    ]
    for copy in scalars:
        copy.start()

    barrier = pltpu.get_barrier_semaphore()
    for d in range(1, n_mp):
        pl.semaphore_signal(barrier, inc=1, device_id={"mp": (m + d) % n_mp}, device_id_type=MESH)
    for d in range(1, n_dp):
        pl.semaphore_signal(barrier, inc=1, device_id={"dp": (g + d) % n_dp}, device_id_type=MESH)
    for d in range(1, n_pack):
        pl.semaphore_signal(
            barrier, inc=1, device_id={"pack": (p + d) % n_pack}, device_id_type=MESH
        )

    text_rows[g] = jnp.zeros((8, 256), F32)
    text_rows[g, :, 0:width] = texts_ref[...].astype(F32)

    pl.semaphore_wait(barrier, n_mp + n_dp + n_pack - 3)

    def remote(src, dst, send, recv, where):
        return pltpu.make_async_remote_copy(
            src_ref=src,
            dst_ref=dst,
            send_sem=send,
            recv_sem=recv,
            device_id=where,
            device_id_type=MESH,
        )

    def own_to_right(s):
        return remote(tile_hbm.at[s], rows.at[s, m], x_send.at[s, 0], x_recv.at[s, 0], {"mp": right})

    def own_to_left(s):
        return remote(tile_hbm.at[s], rows.at[s, m], x_send.at[s, 1], x_recv.at[s, 1], {"mp": left})

    def own_to_twin(s):
        return remote(tile_hbm.at[s], rows.at[s, m], x_send.at[s, 2], x_recv.at[s, 2], {"mp": twin})

    def own_to_far(s):
        return remote(tile_hbm.at[s], rows.at[s, m], x_send.at[s, 3], x_recv.at[s, 3], {"mp": far})

    mid = width // 2

    def pass_right(s):
        part = rows.at[s, left, pl.ds(0, mid)]
        return remote(part, part, x_send.at[s, 6], x_recv.at[s, 6], {"mp": right})

    def pass_left(s):
        part = rows.at[s, right, pl.ds(mid, mid)]
        return remote(part, part, x_send.at[s, 8], x_recv.at[s, 8], {"mp": left})

    def share(s, whose, k):
        part = rows.at[s, whose]
        return remote(part, part, x_send.at[s, k], x_recv.at[s, k], {"mp": twin})

    def got(s, k, part):
        return remote(part, part, x_send.at[s, k], x_recv.at[s, k], {"mp": twin})

    def send_near(s):
        own_to_right(s).start()
        own_to_left(s).start()
        own_to_twin(s).start()

    def take_near(s, hand_on):
        got(s, 0, rows.at[s, left]).wait_recv()
        if hand_on:
            pass_right(s).start()
        share(s, left, 4).start()
        got(s, 1, rows.at[s, right]).wait_recv()
        if hand_on:
            pass_left(s).start()
        share(s, right, 5).start()

    last = SRC - 1
    send_near(0)
    send_near(1)

    def text_copy(d):
        return remote(
            text_rows.at[g], text_rows.at[g], t_send.at[d], t_recv.at[g], {"dp": (g + d) % n_dp}
        )

    for d in far_first(n_dp):
        text_copy(d).start()

    load_proj.wait()
    load_tile.wait()
    for copy in scalars:
        copy.wait()
    pooled[...] = jnp.zeros_like(pooled)

    def attend(s):
        e1 = info_ref[s, 1]
        e2 = e1 + info_ref[s, 2]
        e3 = e2 + info_ref[s, 3]

        def image_of(position):
            return (
                (position >= e1).astype(jnp.int32)
                + (position >= e2).astype(jnp.int32)
                + (position >= e3).astype(jnp.int32)
            )

        image = iota((16, BLK), 0)
        same = image_of(iota((16, BLK), 1)) == image
        query_extra = jnp.where((image < IPB) & same, -1e30, 0.0).astype(BF16)
        key_extra = jnp.where((image < IPB) & jnp.logical_not(same), 1.0, 0.0).astype(BF16)

        features = rows[s].reshape(n_mp * width, BLK)
        projected = dot(proj[...].reshape(3 * width, n_mp * width), features)
        queries = (projected[0:width] * HEAD**-0.5).astype(BF16)
        keys = projected[width : 2 * width].astype(BF16)
        values = projected[2 * width : 3 * width].astype(BF16)

        row16 = iota((SRC * IPB, BLK), 0)
        member = (row16 // IPB == s) & (row16 % IPB == image_of(iota((SRC * IPB, BLK), 1)))
        member = jnp.where(member, 1.0, 0.0).astype(BF16)
        weights = []
        for h in range(width // HEAD):
            head = slice(h * HEAD, (h + 1) * HEAD)
            scores = lax.dot_general(
                jnp.concatenate([keys[head], key_extra], axis=0),
                jnp.concatenate([queries[head], query_extra], axis=0),
                (((0,), (0,)), ((), ())),
                preferred_element_type=F32,
            )
            exponent = jnp.exp(scores - jnp.max(scores, axis=0, keepdims=True))
            inverse = 1.0 / jnp.sum(exponent, axis=0, keepdims=True)
            weights.append(dot_t(member, (exponent * inverse).astype(BF16)))
        hi, lo = split2(jnp.concatenate(weights, axis=0))
        sums = dot_t(hi, values) + dot_t(lo, values)
        col = iota((SRC * IPB, width), 1)
        picked = sums[0 : SRC * IPB]
        for h in range(1, width // HEAD):
            picked = jnp.where(
                col >= h * HEAD, sums[h * SRC * IPB : (h + 1) * SRC * IPB], picked
            )
        pooled[...] += picked

    take_near(0, True)
    send_near(2)
    take_near(1, True)
    send_near(3)

    def slot(s, carry):
        @pl.when(s == 1)
        def _():
            take_near(2, True)
            own_to_far(last).start()

        @pl.when(s == 2)
        def _():
            take_near(last, False)

        @pl.when(s < last)
        def _():
            got(s, 6, rows.at[s, far, pl.ds(0, mid)]).wait_recv()
            got(s, 8, rows.at[s, far, pl.ds(mid, mid)]).wait_recv()

        @pl.when(s == last)
        def _():
            got(s, 3, rows.at[s, far]).wait_recv()

        share(s, far, 7).start()
        for k, offset in ((2, chip), (4, left // 2), (5, right // 2), (7, far // 2)):
            got(s, k, rows.at[s, offset * 2 + 1 - core]).wait_recv()
        attend(s)
        return carry

    lax.fori_loop(0, SRC, slot, 0)

    r = iota((SRC * IPB, 1), 0)
    label = jnp.zeros((SRC * IPB, 1), jnp.int32)
    place = jnp.zeros((SRC * IPB, 1), jnp.int32)
    count = jnp.ones((SRC * IPB, 1), jnp.int32)
    for s in range(SRC):
        for n in range(IPB):
            here = r == s * IPB + n
            label = jnp.where(here, info_ref[s, 1 + IPB + n], label)
            place = jnp.where(here, info_ref[s, 0] * IPB + n, place)
            count = jnp.where(here, info_ref[s, 1 + n], count)
    embeds = (pooled[...] * (1.0 / count.astype(F32))).astype(BF16)
    squares = jnp.sum(embeds.astype(F32) * embeds.astype(F32), axis=1, keepdims=True)
    sq0 = squares.astype(BF16).astype(F32)
    sq1 = (squares - sq0).astype(BF16).astype(F32)
    sq2 = squares - sq0 - sq1
    col = iota((SRC * IPB, 256), 1)
    extended = jnp.zeros((SRC * IPB, 256), F32)
    for at, value in (
        (LABEL_HI, (label // 8).astype(F32)),
        (LABEL_LO, (label % 8).astype(F32)),
        (PLACE, place.astype(F32)),
        (SQ0, sq0),
        (SQ1, sq1),
        (SQ2, sq2),
    ):
        extended = jnp.where(col == at, value, extended)
    pack_rows[p] = extended.astype(BF16)
    pack_rows[p, :, 0:width] = embeds

    def embed_copy(d):
        return remote(
            pack_rows.at[p], pack_rows.at[p], e_send.at[d], e_recv.at[p], {"pack": (p + d) % n_pack}
        )

    for d in far_first(n_pack):
        embed_copy(d).start()

    for d in range(1, n_dp):
        src = (g + d) % n_dp
        remote(
            text_rows.at[src], text_rows.at[src], t_send.at[d], t_recv.at[src], {"dp": src}
        ).wait_recv()
    n_texts = n_dp * text_rows.shape[1]
    text_all = text_rows[...].reshape(n_texts, 256)
    text_all = jnp.where(iota((n_texts, 256), 1) < width, text_all, 0.0)
    text_squares = jnp.sum(text_all * text_all, axis=1, keepdims=True)
    text_bf = text_all.astype(BF16)
    pick = iota((16, 256), 1)
    is_square = (pick >= SQ0) & (pick <= SQ2)
    low = iota((16, 256), 0) < 8
    reads = jnp.where(low & is_square, 1.0, 0.0)
    reads = jnp.where(jnp.logical_not(low) & (pick == LABEL_HI), 8.0, reads)
    reads = jnp.where(jnp.logical_not(low) & (pick == LABEL_LO), 1.0, reads)
    left_side = jnp.concatenate([text_bf, reads.astype(BF16)], axis=0)

    for d in range(1, n_pack):
        src = (p + d) % n_pack
        remote(
            pack_rows.at[src], pack_rows.at[src], e_send.at[d], e_recv.at[src], {"pack": src}
        ).wait_recv()

    n_slots = n_pack * SRC * IPB
    n_images = n_pack * DEST * IPB
    loose = pack_rows[...].reshape(n_slots, 256)
    find = jnp.where(iota((128, 256), 1) == PLACE, 1.0, 0.0).astype(BF16)
    placing = dot_t(find, loose) == iota((128, n_slots), 0).astype(F32)
    packed = dot(jnp.where(placing, 1.0, 0.0).astype(BF16), loose).astype(BF16)

    products = dot_t(left_side, packed)
    image_lane = iota((n_texts, 128), 1)
    sims[m, 0:n_texts, :] = jnp.where(image_lane < n_images, products[0:n_texts], text_squares)
    sims[m, n_texts : n_texts + 8, :] = products[n_texts : n_texts + 8]
    labels = products[n_texts + 8 : n_texts + 9]

    def sims_copy(k):
        to = (far, right, left)[k]
        return remote(sims.at[m], sims.at[m], s_send.at[k], s_recv.at[k], {"mp": to})

    for k in range(3):
        sims_copy(k).start()
    text_row = iota((n_texts, 128), 0)
    matching = labels == (((text_row // 8) * n_pack + p) * 8 + text_row % 8).astype(F32)
    sign = jnp.where(matching, 1.0, -1.0)
    for k, src in enumerate((far, left, right)):
        remote(sims.at[src], sims.at[src], s_send.at[k], s_recv.at[k], {"mp": src}).wait_recv()
    halves[core] = (sims[core] + sims[2 + core]) + (sims[4 + core] + sims[6 + core])
    half_copy = remote(
        halves.at[core], halves.at[core], s_send.at[3], s_recv.at[3], {"mp": twin}
    )
    half_copy.start()
    half_copy.wait_recv()
    total = halves[0] + halves[1]
    cosine = total[0:n_texts]
    image_scale = lax.rsqrt(total[n_texts : n_texts + 1] + 1e-06)
    text_scale = lax.rsqrt(
        jnp.sum(jnp.where(image_lane == n_images, cosine, 0.0), axis=1, keepdims=True) + 1e-06
    )
    heat = heat_ref[0]
    logits = heat * cosine * image_scale * text_scale + shift_ref[0]
    slopes = -sign * jax.nn.sigmoid(-sign * logits) * heat
    slopes = jnp.where(image_lane < n_images, slopes, 0.0)

    hi, lo = split2(slopes * text_scale)
    contract0 = (((0,), (0,)), ((), ()))
    image_part = lax.dot_general(hi, text_bf, contract0, preferred_element_type=F32)
    image_part += lax.dot_general(lo, text_bf, contract0, preferred_element_type=F32)
    own_image[...] = image_part[0:n_images].reshape(n_pack, 8, 256)

    def image_copy(d):
        to = (p + d) % n_pack
        return remote(
            own_image.at[to], image_terms.at[p], iz_send.at[d], iz_recv.at[p], {"pack": to}
        )

    for d in far_first(n_pack):
        image_copy(d).start()

    hi, lo = split2(slopes * jnp.where(iota((1, 128), 1) < n_images, image_scale, 0.0))
    text_part = dot(hi, packed) + dot(lo, packed)
    own_text[...] = text_part.reshape(n_dp, 8, 256)

    def text_term_copy(d):
        to = (g + d) % n_dp
        return remote(own_text.at[to], text_terms.at[g], ty_send.at[d], ty_recv.at[g], {"dp": to})

    for d in far_first(n_dp):
        text_term_copy(d).start()

    image_terms[p] = own_image[p]
    text_terms[g] = own_text[g]
    for d in range(1, n_dp):
        src = (g + d) % n_dp
        remote(
            own_text.at[src], text_terms.at[src], ty_send.at[d], ty_recv.at[src], {"dp": src}
        ).wait_recv()
    text_out[...] = jnp.sum(text_terms[...], axis=0)[:, 0:width]
    for d in range(1, n_pack):
        src = (p + d) % n_pack
        remote(
            own_image.at[src], image_terms.at[src], iz_send.at[d], iz_recv.at[src], {"pack": src}
        ).wait_recv()
    image_out[...] = jnp.sum(image_terms[...], axis=0)[:, 0:width]

    for s in range(SRC):
        own_to_right(s).wait_send()
        own_to_left(s).wait_send()
        own_to_twin(s).wait_send()
        share(s, left, 4).wait_send()
        share(s, right, 5).wait_send()
        share(s, far, 7).wait_send()
        if s < last:
            pass_right(s).wait_send()
            pass_left(s).wait_send()
        else:
            own_to_far(s).wait_send()
    for d in range(1, n_dp):
        text_copy(d).wait_send()
        text_term_copy(d).wait_send()
    for d in range(1, n_pack):
        embed_copy(d).wait_send()
        image_copy(d).wait_send()
    for k in range(3):
        sims_copy(k).wait_send()
    half_copy.wait_send()


def on_device(
    n_dp,
    n_pack,
    n_mp,
    tile_activity,
    tokens_per_picture,
    slot_destinations,
    caption_indices,
    attention_projections,
    caption_vectors,
    score_inverse_heat,
    score_shift,
):
    width = caption_vectors.shape[1]
    depth = attention_projections.shape[1]
    n_texts = n_dp * caption_vectors.shape[0]
    block_info = jnp.concatenate(
        [slot_destinations[:, None], tokens_per_picture, caption_indices], axis=1
    )
    vmem = pl.BlockSpec(memory_space=pltpu.VMEM)
    hbm = pl.BlockSpec(memory_space=pltpu.HBM)
    dma = pltpu.SemaphoreType.DMA
    return pl.pallas_call(
        functools.partial(kernel, n_dp, n_pack, n_mp),
        out_shape=(
            jax.ShapeDtypeStruct(caption_vectors.shape, F32),
            jax.ShapeDtypeStruct(caption_vectors.shape, F32),
        ),
        in_specs=[hbm, hbm, hbm, vmem, hbm, hbm],
        out_specs=(vmem, vmem),
        scratch_shapes=[
            pltpu.SMEM(block_info.shape, jnp.int32),
            pltpu.SMEM((1,), F32),
            pltpu.SMEM((1,), F32),
            pltpu.VMEM((3, width, depth), BF16),
            pltpu.VMEM((SRC, n_mp, width, BLK), BF16),
            pltpu.VMEM((SRC * IPB, width), F32),
            pltpu.VMEM((n_dp, 8, 256), F32),
            pltpu.VMEM((n_pack, SRC * IPB, 256), BF16),
            pltpu.VMEM((n_mp, n_texts + 8, 128), F32),
            pltpu.VMEM((2, n_texts + 8, 128), F32),
            pltpu.VMEM((n_dp, 8, 256), F32),
            pltpu.VMEM((n_pack, 8, 256), F32),
            pltpu.VMEM((n_dp, 8, 256), F32),
            pltpu.VMEM((n_pack, 8, 256), F32),
            dma((5,)),
            dma((SRC, 9)),
            dma((SRC, 9)),
            dma((n_dp,)),
            dma((n_dp,)),
            dma((n_pack,)),
            dma((n_pack,)),
            dma((4,)),
            dma((4,)),
            dma((n_dp,)),
            dma((n_dp,)),
            dma((n_pack,)),
            dma((n_pack,)),
        ],
        compiler_params=pltpu.CompilerParams(
            collective_id=0, has_side_effects=True, vmem_limit_bytes=55040 * 1024
        ),
        name="contrastive_step",
    )(
        jnp.swapaxes(tile_activity, 1, 2),
        block_info,
        jnp.swapaxes(attention_projections, 1, 2),
        caption_vectors,
        score_inverse_heat,
        score_shift,
    )


def solution(mesh):
    sizes = (mesh.shape["dp"], mesh.shape["pack"], mesh.shape["mp"])
    return jax.shard_map(
        functools.partial(on_device, *sizes),
        mesh=mesh,
        in_specs=(
            P(("dp", "pack"), None, "mp"),
            P(("dp", "pack"), None),
            P(("dp", "pack")),
            P(("dp", "pack"), None),
            P(None, None, "mp"),
            P(("dp", "pack"), "mp"),
            P(),
            P(),
        ),
        out_specs=(P(("dp", "pack"), "mp"), P(("dp", "pack"), "mp")),
        check_vma=False,
    )
```

```python
import functools

import jax
import jax.numpy as jnp
from jax import lax
from jax.experimental import pallas as pl
from jax.experimental.pallas import tpu as pltpu
from jax.sharding import PartitionSpec as P

HEAD = 64
BLK = 256
IPB = 4
DEST = 2
SRC = 4
F32 = jnp.float32
BF16 = jnp.bfloat16
MESH = pl.DeviceIdType.MESH

LABEL_HI, LABEL_LO, PLACE, SQ0, SQ1, SQ2 = 192, 193, 194, 195, 196, 197


def dot(a, b):
    return jnp.dot(a, b, preferred_element_type=F32)


def dot_t(a, b):
    return lax.dot_general(a, b, (((1,), (1,)), ((), ())), preferred_element_type=F32)


def iota(shape, axis):
    return lax.broadcasted_iota(jnp.int32, shape, axis)


def split2(a):
    hi = a.astype(BF16)
    return hi, (a - hi.astype(F32)).astype(BF16)


def far_first(n):
    return sorted(range(1, n), key=lambda d: -min(d, n - d))


def kernel(
    n_dp,
    n_pack,
    n_mp,
    tile_hbm,
    info_hbm,
    proj_hbm,
    texts_ref,
    heat_hbm,
    shift_hbm,
    image_out,
    text_out,
    info_ref,
    heat_ref,
    shift_ref,
    proj,
    rows,
    pooled,
    text_rows,
    pack_rows,
    late_rows,
    marks,
    inverse_count,
    sims,
    halves,
    own_text,
    own_image,
    text_terms,
    image_terms,
    load_sem,
    x_send,
    x_recv,
    t_send,
    t_recv,
    e_send,
    e_recv,
    l_send,
    l_recv,
    s_send,
    s_recv,
    ty_send,
    ty_recv,
    iz_send,
    iz_recv,
):
    g, p, m = lax.axis_index("dp"), lax.axis_index("pack"), lax.axis_index("mp")
    chips = n_mp // 2
    chip, core = m // 2, m % 2
    right = ((chip + 1) % chips) * 2 + core
    left = ((chip + chips - 1) % chips) * 2 + core
    far = ((chip + 2) % chips) * 2 + core
    twin = chip * 2 + 1 - core
    width = texts_ref.shape[1]

    load_tile = pltpu.make_async_copy(tile_hbm, rows.at[:, m], load_sem.at[0])
    load_proj = pltpu.make_async_copy(proj_hbm, proj, load_sem.at[1])
    load_tile.start()
    load_proj.start()
    scalars = [
        pltpu.make_async_copy(src, dst, load_sem.at[2 + i])
        for i, (src, dst) in enumerate(
            (
                (info_hbm, info_ref),
                (heat_hbm, heat_ref),
                (shift_hbm, shift_ref),
            )
        )
    ]
    for copy in scalars:
        copy.start()

    barrier = pltpu.get_barrier_semaphore()
    for d in range(1, n_mp):
        pl.semaphore_signal(barrier, inc=1, device_id={"mp": (m + d) % n_mp}, device_id_type=MESH)
    for d in range(1, n_dp):
        pl.semaphore_signal(barrier, inc=1, device_id={"dp": (g + d) % n_dp}, device_id_type=MESH)
    for d in range(1, n_pack):
        pl.semaphore_signal(
            barrier, inc=1, device_id={"pack": (p + d) % n_pack}, device_id_type=MESH
        )

    text_rows[g] = jnp.zeros((8, 256), F32)
    text_rows[g, :, 0:width] = texts_ref[...].astype(F32)

    pl.semaphore_wait(barrier, n_mp + n_dp + n_pack - 3)

    def remote(src, dst, send, recv, where):
        return pltpu.make_async_remote_copy(
            src_ref=src,
            dst_ref=dst,
            send_sem=send,
            recv_sem=recv,
            device_id=where,
            device_id_type=MESH,
        )

    def own_to_right(s):
        return remote(tile_hbm.at[s], rows.at[s, m], x_send.at[s, 0], x_recv.at[s, 0], {"mp": right})

    def own_to_left(s):
        return remote(tile_hbm.at[s], rows.at[s, m], x_send.at[s, 1], x_recv.at[s, 1], {"mp": left})

    def own_to_twin(s):
        return remote(tile_hbm.at[s], rows.at[s, m], x_send.at[s, 2], x_recv.at[s, 2], {"mp": twin})

    def own_to_far(s):
        return remote(tile_hbm.at[s], rows.at[s, m], x_send.at[s, 3], x_recv.at[s, 3], {"mp": far})

    mid = width // 2

    def pass_right(s):
        part = rows.at[s, left, pl.ds(0, mid)]
        return remote(part, part, x_send.at[s, 6], x_recv.at[s, 6], {"mp": right})

    def pass_left(s):
        part = rows.at[s, right, pl.ds(mid, mid)]
        return remote(part, part, x_send.at[s, 8], x_recv.at[s, 8], {"mp": left})

    def share(s, whose, k):
        part = rows.at[s, whose]
        return remote(part, part, x_send.at[s, k], x_recv.at[s, k], {"mp": twin})

    def got(s, k, part):
        return remote(part, part, x_send.at[s, k], x_recv.at[s, k], {"mp": twin})

    def send_near(s):
        own_to_right(s).start()
        own_to_left(s).start()
        own_to_twin(s).start()

    def take_near(s, hand_on):
        got(s, 0, rows.at[s, left]).wait_recv()
        if hand_on:
            pass_right(s).start()
        share(s, left, 4).start()
        got(s, 1, rows.at[s, right]).wait_recv()
        if hand_on:
            pass_left(s).start()
        share(s, right, 5).start()

    last = SRC - 1
    send_near(0)
    send_near(1)

    def text_copy(d):
        return remote(
            text_rows.at[g], text_rows.at[g], t_send.at[d], t_recv.at[g], {"dp": (g + d) % n_dp}
        )

    for d in far_first(n_dp):
        text_copy(d).start()

    load_proj.wait()
    load_tile.wait()
    for copy in scalars:
        copy.wait()
    pooled[...] = jnp.zeros_like(pooled)

    def project(s, whose):
        weights = [
            proj[:, :, pl.ds(pl.multiple_of(c * 2 * width, 128), 2 * width)] for c in whose
        ]
        features = [rows[s, pl.ds(c * 2, 2)].reshape(2 * width, BLK) for c in whose]
        return dot(
            jnp.concatenate(weights, axis=2).reshape(3 * width, len(whose) * 2 * width),
            jnp.concatenate(features, axis=0),
        )

    def attend(s, projected):
        e1 = info_ref[s, 0]
        e2 = e1 + info_ref[s, 1]
        e3 = e2 + info_ref[s, 2]

        def image_of(position):
            return (
                (position >= e1).astype(jnp.int32)
                + (position >= e2).astype(jnp.int32)
                + (position >= e3).astype(jnp.int32)
            )

        image = iota((16, BLK), 0)
        same = image_of(iota((16, BLK), 1)) == image
        query_extra = jnp.where((image < IPB) & same, -1e30, 0.0).astype(BF16)
        key_extra = jnp.where((image < IPB) & jnp.logical_not(same), 1.0, 0.0).astype(BF16)

        queries = (projected[0:width] * HEAD**-0.5).astype(BF16)
        keys = projected[width : 2 * width].astype(BF16)
        values = projected[2 * width : 3 * width].astype(BF16)

        row16 = iota((SRC * IPB, BLK), 0)
        member = (row16 // IPB == s) & (row16 % IPB == image_of(iota((SRC * IPB, BLK), 1)))
        member = jnp.where(member, 1.0, 0.0).astype(BF16)
        weights = []
        for h in range(width // HEAD):
            head = slice(h * HEAD, (h + 1) * HEAD)
            scores = lax.dot_general(
                jnp.concatenate([keys[head], key_extra], axis=0),
                jnp.concatenate([queries[head], query_extra], axis=0),
                (((0,), (0,)), ((), ())),
                preferred_element_type=F32,
            )
            exponent = jnp.exp(scores - jnp.max(scores, axis=0, keepdims=True))
            inverse = 1.0 / jnp.sum(exponent, axis=0, keepdims=True)
            weights.append(dot_t(member, (exponent * inverse).astype(BF16)))
        hi, lo = split2(jnp.concatenate(weights, axis=0))
        sums = dot_t(hi, values) + dot_t(lo, values)
        out_col = iota((SRC * IPB, width), 1)
        picked = sums[0 : SRC * IPB]
        for h in range(1, width // HEAD):
            picked = jnp.where(
                out_col >= h * HEAD, sums[h * SRC * IPB : (h + 1) * SRC * IPB], picked
            )
        pooled[:, 0:width] += picked

    take_near(0, True)
    send_near(2)
    take_near(1, True)
    send_near(3)
    own_to_far(last).start()

    r = iota((SRC * IPB, 1), 0)
    label = jnp.zeros((SRC * IPB, 1), jnp.int32)
    place = jnp.zeros((SRC * IPB, 1), jnp.int32)
    count = jnp.ones((SRC * IPB, 1), jnp.int32)
    for k in range(SRC):
        for n in range(IPB):
            here = r == k * IPB + n
            label = jnp.where(here, info_ref[SRC + k, n], label)
            place = jnp.where(here, info_ref[0, IPB + k] * IPB + n, place)
            count = jnp.where(here, info_ref[k, n], count)
    inverse_count[...] = jnp.broadcast_to(1.0 / count.astype(F32), inverse_count.shape)
    col = iota((SRC * IPB, 256), 1)
    marks[...] = jnp.zeros_like(marks)
    for at, value in ((LABEL_HI, label // 8), (LABEL_LO, label % 8), (PLACE, place)):
        marks[...] = jnp.where(col == at, value.astype(F32), marks[...])

    def image_rows():
        means = (pooled[...] * inverse_count[...]).astype(BF16).astype(F32)
        squares = jnp.sum(means * means, axis=1, keepdims=True)
        sq0 = squares.astype(BF16).astype(F32)
        sq1 = (squares - sq0).astype(BF16).astype(F32)
        extended = jnp.where(col == SQ0, sq0, 0.0)
        extended = jnp.where(col == SQ1, sq1, extended)
        return jnp.where(
            col < width, means, jnp.where(col == SQ2, squares - sq0 - sq1, extended)
        )

    def embed_copy(d):
        return remote(
            pack_rows.at[p], pack_rows.at[p], e_send.at[d], e_recv.at[p], {"pack": (p + d) % n_pack}
        )

    def slot(s, carry):
        @pl.when(s == 1)
        def _():
            take_near(2, True)

        @pl.when(s == 2)
        def _():
            take_near(last, False)

        @pl.when(s < last)
        def _():
            got(s, 6, rows.at[s, far, pl.ds(0, mid)]).wait_recv()
            got(s, 8, rows.at[s, far, pl.ds(mid, mid)]).wait_recv()

        @pl.when(s == last)
        def _():
            got(s, 3, rows.at[s, far]).wait_recv()

        share(s, far, 7).start()

        @pl.when(s == last)
        def _():
            pack_rows[p] = (image_rows() + marks[...]).astype(BF16)
            for d in far_first(n_pack):
                embed_copy(d).start()

        for k, whose in ((2, chip), (4, left // 2), (5, right // 2)):
            got(s, k, rows.at[s, whose * 2 + 1 - core]).wait_recv()
        near = project(s, (chip, left // 2, right // 2))
        got(s, 7, rows.at[s, far + 1 - 2 * core]).wait_recv()
        attend(s, near + project(s, (far // 2,)))
        return carry

    lax.fori_loop(0, SRC, slot, 0)

    whole = image_rows()
    late_rows[p, 0:IPB, :] = whole[last * IPB :, 0:128]
    late_rows[p, IPB : 2 * IPB, :] = whole[last * IPB :, 128:256]

    def late_copy(d):
        return remote(
            late_rows.at[p], late_rows.at[p], l_send.at[d], l_recv.at[p], {"pack": (p + d) % n_pack}
        )

    for d in far_first(n_pack):
        late_copy(d).start()

    for d in range(1, n_dp):
        src = (g + d) % n_dp
        remote(
            text_rows.at[src], text_rows.at[src], t_send.at[d], t_recv.at[src], {"dp": src}
        ).wait_recv()
    n_texts = n_dp * text_rows.shape[1]
    text_all = text_rows[...].reshape(n_texts, 256)
    text_all = jnp.where(iota((n_texts, 256), 1) < width, text_all, 0.0)
    text_squares = jnp.sum(text_all * text_all, axis=1, keepdims=True)
    text_bf = text_all.astype(BF16)
    pick = iota((16, 256), 1)
    is_square = (pick >= SQ0) & (pick <= SQ2)
    low = iota((16, 256), 0) < 8
    reads = jnp.where(low & is_square, 1.0, 0.0)
    reads = jnp.where(jnp.logical_not(low) & (pick == LABEL_HI), 8.0, reads)
    reads = jnp.where(jnp.logical_not(low) & (pick == LABEL_LO), 1.0, reads)
    left_side = jnp.concatenate([text_bf, reads.astype(BF16)], axis=0)

    for d in range(1, n_pack):
        src = (p + d) % n_pack
        remote(
            pack_rows.at[src], pack_rows.at[src], e_send.at[d], e_recv.at[src], {"pack": src}
        ).wait_recv()

    n_slots = n_pack * SRC * IPB
    n_images = n_pack * DEST * IPB
    loose = pack_rows[...].reshape(n_slots, 256)
    find = jnp.where(iota((128, 256), 1) == PLACE, 1.0, 0.0).astype(BF16)
    placing = dot_t(find, loose) == iota((128, n_slots), 0).astype(F32)
    placing = jnp.where(placing, 1.0, 0.0).astype(BF16)
    early = dot(placing, loose)
    slot_row = iota((n_slots, n_pack * 8), 0)
    late_row = iota((n_slots, n_pack * 8), 1)
    pair = (slot_row // 16 == late_row // 8) & (slot_row % 16 >= last * IPB)
    pair = pair & (slot_row % IPB == late_row % IPB)
    first = late_row % 8 < IPB
    first_placing = dot(placing, jnp.where(pair & first, 1.0, 0.0).astype(BF16)).astype(BF16)
    second_placing = dot(placing, jnp.where(pair & jnp.logical_not(first), 1.0, 0.0).astype(BF16))
    second_placing = second_placing.astype(BF16)

    for d in range(1, n_pack):
        src = (p + d) % n_pack
        remote(
            late_rows.at[src], late_rows.at[src], l_send.at[d], l_recv.at[src], {"pack": src}
        ).wait_recv()
    late = late_rows[...].reshape(n_pack * 8, 128).astype(BF16)
    late = jnp.concatenate([dot(first_placing, late), dot(second_placing, late)], axis=1)
    packed = (early + late).astype(BF16)

    products = dot_t(left_side, packed)
    image_lane = iota((n_texts, 128), 1)
    sims[m, 0:n_texts, :] = jnp.where(image_lane < n_images, products[0:n_texts], text_squares)
    sims[m, n_texts : n_texts + 8, :] = products[n_texts : n_texts + 8]
    labels = products[n_texts + 8 : n_texts + 9]

    def sims_copy(k):
        to = (far, right, left)[k]
        return remote(sims.at[m], sims.at[m], s_send.at[k], s_recv.at[k], {"mp": to})

    for k in range(3):
        sims_copy(k).start()
    text_row = iota((n_texts, 128), 0)
    matching = labels == (((text_row // 8) * n_pack + p) * 8 + text_row % 8).astype(F32)
    sign = jnp.where(matching, 1.0, -1.0)
    for k, src in enumerate((far, left, right)):
        remote(sims.at[src], sims.at[src], s_send.at[k], s_recv.at[k], {"mp": src}).wait_recv()
    halves[core] = (sims[core] + sims[2 + core]) + (sims[4 + core] + sims[6 + core])
    half_copy = remote(
        halves.at[core], halves.at[core], s_send.at[3], s_recv.at[3], {"mp": twin}
    )
    half_copy.start()
    half_copy.wait_recv()
    total = halves[0] + halves[1]
    cosine = total[0:n_texts]
    image_scale = lax.rsqrt(total[n_texts : n_texts + 1] + 1e-06)
    text_scale = lax.rsqrt(
        jnp.sum(jnp.where(image_lane == n_images, cosine, 0.0), axis=1, keepdims=True) + 1e-06
    )
    heat = heat_ref[0]
    logits = heat * cosine * image_scale * text_scale + shift_ref[0]
    slopes = -sign * jax.nn.sigmoid(-sign * logits) * heat
    slopes = jnp.where(image_lane < n_images, slopes, 0.0)

    hi, lo = split2(slopes * text_scale)
    contract0 = (((0,), (0,)), ((), ()))
    image_part = lax.dot_general(hi, text_bf, contract0, preferred_element_type=F32)
    image_part += lax.dot_general(lo, text_bf, contract0, preferred_element_type=F32)
    own_image[...] = image_part[0:n_images].reshape(n_pack, 8, 256)

    def image_copy(d):
        to = (p + d) % n_pack
        return remote(
            own_image.at[to], image_terms.at[p], iz_send.at[d], iz_recv.at[p], {"pack": to}
        )

    for d in far_first(n_pack):
        image_copy(d).start()

    hi, lo = split2(slopes * jnp.where(iota((1, 128), 1) < n_images, image_scale, 0.0))
    text_part = dot(hi, packed) + dot(lo, packed)
    own_text[...] = text_part.reshape(n_dp, 8, 256)

    def text_term_copy(d):
        to = (g + d) % n_dp
        return remote(own_text.at[to], text_terms.at[g], ty_send.at[d], ty_recv.at[g], {"dp": to})

    for d in far_first(n_dp):
        text_term_copy(d).start()

    image_terms[p] = own_image[p]
    text_terms[g] = own_text[g]
    for d in range(1, n_dp):
        src = (g + d) % n_dp
        remote(
            own_text.at[src], text_terms.at[src], ty_send.at[d], ty_recv.at[src], {"dp": src}
        ).wait_recv()
    text_out[...] = jnp.sum(text_terms[...], axis=0)[:, 0:width]
    for d in range(1, n_pack):
        src = (p + d) % n_pack
        remote(
            own_image.at[src], image_terms.at[src], iz_send.at[d], iz_recv.at[src], {"pack": src}
        ).wait_recv()
    image_out[...] = jnp.sum(image_terms[...], axis=0)[:, 0:width]

    for s in range(SRC):
        own_to_right(s).wait_send()
        own_to_left(s).wait_send()
        own_to_twin(s).wait_send()
        share(s, left, 4).wait_send()
        share(s, right, 5).wait_send()
        share(s, far, 7).wait_send()
        if s < last:
            pass_right(s).wait_send()
            pass_left(s).wait_send()
        else:
            own_to_far(s).wait_send()
    for d in range(1, n_dp):
        text_copy(d).wait_send()
        text_term_copy(d).wait_send()
    for d in range(1, n_pack):
        embed_copy(d).wait_send()
        late_copy(d).wait_send()
        image_copy(d).wait_send()
    for k in range(3):
        sims_copy(k).wait_send()
    half_copy.wait_send()


def on_device(
    n_dp,
    n_pack,
    n_mp,
    tile_activity,
    tokens_per_picture,
    slot_destinations,
    caption_indices,
    attention_projections,
    caption_vectors,
    score_inverse_heat,
    score_shift,
):
    width = caption_vectors.shape[1]
    depth = attention_projections.shape[1]
    n_texts = n_dp * caption_vectors.shape[0]
    block_info = jnp.pad(tokens_per_picture, ((0, SRC), (0, 128 - IPB)))
    block_info += jnp.pad(caption_indices, ((SRC, 0), (0, 128 - IPB)))
    block_info += jnp.pad(slot_destinations[None, :], ((0, 2 * SRC - 1), (IPB, 128 - IPB - SRC)))
    vmem = pl.BlockSpec(memory_space=pltpu.VMEM)
    hbm = pl.BlockSpec(memory_space=pltpu.HBM)
    dma = pltpu.SemaphoreType.DMA
    return pl.pallas_call(
        functools.partial(kernel, n_dp, n_pack, n_mp),
        out_shape=(
            jax.ShapeDtypeStruct(caption_vectors.shape, F32),
            jax.ShapeDtypeStruct(caption_vectors.shape, F32),
        ),
        in_specs=[hbm, hbm, hbm, vmem, hbm, hbm],
        out_specs=(vmem, vmem),
        scratch_shapes=[
            pltpu.SMEM(block_info.shape, jnp.int32),
            pltpu.SMEM((1,), F32),
            pltpu.SMEM((1,), F32),
            pltpu.VMEM((3, width, depth), BF16),
            pltpu.VMEM((SRC, n_mp, width, BLK), BF16),
            pltpu.VMEM((SRC * IPB, 256), F32),
            pltpu.VMEM((n_dp, 8, 256), F32),
            pltpu.VMEM((n_pack, SRC * IPB, 256), BF16),
            pltpu.VMEM((n_pack, 8, 128), F32),
            pltpu.VMEM((SRC * IPB, 256), F32),
            pltpu.VMEM((SRC * IPB, 256), F32),
            pltpu.VMEM((n_mp, n_texts + 8, 128), F32),
            pltpu.VMEM((2, n_texts + 8, 128), F32),
            pltpu.VMEM((n_dp, 8, 256), F32),
            pltpu.VMEM((n_pack, 8, 256), F32),
            pltpu.VMEM((n_dp, 8, 256), F32),
            pltpu.VMEM((n_pack, 8, 256), F32),
            dma((5,)),
            dma((SRC, 9)),
            dma((SRC, 9)),
            dma((n_dp,)),
            dma((n_dp,)),
            dma((n_pack,)),
            dma((n_pack,)),
            dma((n_pack,)),
            dma((n_pack,)),
            dma((4,)),
            dma((4,)),
            dma((n_dp,)),
            dma((n_dp,)),
            dma((n_pack,)),
            dma((n_pack,)),
        ],
        compiler_params=pltpu.CompilerParams(
            collective_id=0, has_side_effects=True, vmem_limit_bytes=55040 * 1024
        ),
        name="contrastive_step",
    )(
        jnp.swapaxes(tile_activity, 1, 2),
        block_info,
        jnp.swapaxes(attention_projections, 1, 2),
        caption_vectors,
        score_inverse_heat,
        score_shift,
    )


def solution(mesh):
    sizes = (mesh.shape["dp"], mesh.shape["pack"], mesh.shape["mp"])
    return jax.shard_map(
        functools.partial(on_device, *sizes),
        mesh=mesh,
        in_specs=(
            P(("dp", "pack"), None, "mp"),
            P(("dp", "pack"), None),
            P(("dp", "pack")),
            P(("dp", "pack"), None),
            P(None, None, "mp"),
            P(("dp", "pack"), "mp"),
            P(),
            P(),
        ),
        out_specs=(P(("dp", "pack"), "mp"), P(("dp", "pack"), "mp")),
        check_vma=False,
    )
```

```python
import functools

import jax
import jax.numpy as jnp
from jax import lax
from jax.experimental import pallas as pl
from jax.experimental.pallas import tpu as pltpu
from jax.sharding import PartitionSpec as P

HEAD = 64
BLK = 256
IPB = 4
DEST = 2
SRC = 4
F32 = jnp.float32
BF16 = jnp.bfloat16
MESH = pl.DeviceIdType.MESH

LABEL_HI, LABEL_LO, PLACE, SQ0, SQ1, SQ2 = 192, 193, 194, 195, 196, 197


def dot(a, b):
    return jnp.dot(a, b, preferred_element_type=F32)


def dot_t(a, b):
    return lax.dot_general(a, b, (((1,), (1,)), ((), ())), preferred_element_type=F32)


def iota(shape, axis):
    return lax.broadcasted_iota(jnp.int32, shape, axis)


def split2(a):
    hi = a.astype(BF16)
    return hi, (a - hi.astype(F32)).astype(BF16)


def far_first(n):
    return sorted(range(1, n), key=lambda d: -min(d, n - d))


def kernel(
    n_dp,
    n_pack,
    n_mp,
    tile_hbm,
    info_hbm,
    proj_hbm,
    texts_ref,
    heat_hbm,
    shift_hbm,
    out,
    info_ref,
    heat_ref,
    shift_ref,
    proj,
    rows,
    pooled,
    text_rows,
    pack_rows,
    late_rows,
    marks,
    inverse_count,
    sims,
    halves,
    own_text,
    own_image,
    text_terms,
    image_terms,
    load_sem,
    x_send,
    x_recv,
    t_send,
    t_recv,
    e_send,
    e_recv,
    l_send,
    l_recv,
    s_send,
    s_recv,
    ty_send,
    ty_recv,
    iz_send,
    iz_recv,
):
    g, p, m = lax.axis_index("dp"), lax.axis_index("pack"), lax.axis_index("mp")
    chips = n_mp // 2
    chip, core = m // 2, m % 2
    right = ((chip + 1) % chips) * 2 + core
    left = ((chip + chips - 1) % chips) * 2 + core
    far = ((chip + 2) % chips) * 2 + core
    twin = chip * 2 + 1 - core
    width = texts_ref.shape[1]

    load_tile = pltpu.make_async_copy(tile_hbm, rows.at[:, m], load_sem.at[0])
    load_proj = pltpu.make_async_copy(proj_hbm, proj, load_sem.at[1])
    load_tile.start()
    load_proj.start()
    scalars = [
        pltpu.make_async_copy(src, dst, load_sem.at[2 + i])
        for i, (src, dst) in enumerate(
            (
                (info_hbm, info_ref),
                (heat_hbm, heat_ref),
                (shift_hbm, shift_ref),
            )
        )
    ]
    for copy in scalars:
        copy.start()

    barrier = pltpu.get_barrier_semaphore()
    for d in range(1, n_mp):
        pl.semaphore_signal(barrier, inc=1, device_id={"mp": (m + d) % n_mp}, device_id_type=MESH)
    for d in range(1, n_dp):
        pl.semaphore_signal(barrier, inc=1, device_id={"dp": (g + d) % n_dp}, device_id_type=MESH)
    for d in range(1, n_pack):
        pl.semaphore_signal(
            barrier, inc=1, device_id={"pack": (p + d) % n_pack}, device_id_type=MESH
        )

    text_rows[g] = jnp.zeros((8, 256), F32)
    text_rows[g, :, 0:width] = texts_ref[...].astype(F32)

    pl.semaphore_wait(barrier, n_mp + n_dp + n_pack - 3)

    def remote(src, dst, send, recv, where):
        return pltpu.make_async_remote_copy(
            src_ref=src,
            dst_ref=dst,
            send_sem=send,
            recv_sem=recv,
            device_id=where,
            device_id_type=MESH,
        )

    def own_to_right(s):
        return remote(tile_hbm.at[s], rows.at[s, m], x_send.at[s, 0], x_recv.at[s, 0], {"mp": right})

    def own_to_left(s):
        return remote(tile_hbm.at[s], rows.at[s, m], x_send.at[s, 1], x_recv.at[s, 1], {"mp": left})

    def own_to_twin(s):
        return remote(tile_hbm.at[s], rows.at[s, m], x_send.at[s, 2], x_recv.at[s, 2], {"mp": twin})

    def own_to_far(s):
        return remote(tile_hbm.at[s], rows.at[s, m], x_send.at[s, 3], x_recv.at[s, 3], {"mp": far})

    mid = width // 2

    def pass_right(s):
        part = rows.at[s, left, pl.ds(0, mid)]
        return remote(part, part, x_send.at[s, 6], x_recv.at[s, 6], {"mp": right})

    def pass_left(s):
        part = rows.at[s, right, pl.ds(mid, mid)]
        return remote(part, part, x_send.at[s, 8], x_recv.at[s, 8], {"mp": left})

    def share(s, whose, k):
        part = rows.at[s, whose]
        return remote(part, part, x_send.at[s, k], x_recv.at[s, k], {"mp": twin})

    def got(s, k, part):
        return remote(part, part, x_send.at[s, k], x_recv.at[s, k], {"mp": twin})

    def send_near(s):
        own_to_right(s).start()
        own_to_left(s).start()
        own_to_twin(s).start()

    def take_near(s, hand_on):
        got(s, 0, rows.at[s, left]).wait_recv()
        if hand_on:
            pass_right(s).start()
        share(s, left, 4).start()
        got(s, 1, rows.at[s, right]).wait_recv()
        if hand_on:
            pass_left(s).start()
        share(s, right, 5).start()

    last = SRC - 1
    send_near(0)
    send_near(1)

    def text_copy(d):
        return remote(
            text_rows.at[g], text_rows.at[g], t_send.at[d], t_recv.at[g], {"dp": (g + d) % n_dp}
        )

    for d in far_first(n_dp):
        text_copy(d).start()

    load_proj.wait()
    load_tile.wait()
    for copy in scalars:
        copy.wait()
    pooled[...] = jnp.zeros_like(pooled)

    def project(s, whose):
        weights = [
            proj[:, :, pl.ds(pl.multiple_of(c * 2 * width, 128), 2 * width)] for c in whose
        ]
        features = [rows[s, pl.ds(c * 2, 2)].reshape(2 * width, BLK) for c in whose]
        return dot(
            jnp.concatenate(weights, axis=2).reshape(3 * width, len(whose) * 2 * width),
            jnp.concatenate(features, axis=0),
        )

    def attend(s, projected):
        e1 = info_ref[s, 0]
        e2 = e1 + info_ref[s, 1]
        e3 = e2 + info_ref[s, 2]

        def image_of(position):
            return (
                (position >= e1).astype(jnp.int32)
                + (position >= e2).astype(jnp.int32)
                + (position >= e3).astype(jnp.int32)
            )

        image = iota((16, BLK), 0)
        same = image_of(iota((16, BLK), 1)) == image
        query_extra = jnp.where((image < IPB) & same, -1e30, 0.0).astype(BF16)
        key_extra = jnp.where((image < IPB) & jnp.logical_not(same), 1.0, 0.0).astype(BF16)

        queries = (projected[0:width] * HEAD**-0.5).astype(BF16)
        keys = projected[width : 2 * width].astype(BF16)
        values = projected[2 * width : 3 * width].astype(BF16)

        row16 = iota((SRC * IPB, BLK), 0)
        member = (row16 // IPB == s) & (row16 % IPB == image_of(iota((SRC * IPB, BLK), 1)))
        member = jnp.where(member, 1.0, 0.0).astype(BF16)
        weights = []
        for h in range(width // HEAD):
            head = slice(h * HEAD, (h + 1) * HEAD)
            scores = lax.dot_general(
                jnp.concatenate([keys[head], key_extra], axis=0),
                jnp.concatenate([queries[head], query_extra], axis=0),
                (((0,), (0,)), ((), ())),
                preferred_element_type=F32,
            )
            exponent = jnp.exp(scores - jnp.max(scores, axis=0, keepdims=True))
            inverse = 1.0 / jnp.sum(exponent, axis=0, keepdims=True)
            weights.append(dot_t(member, (exponent * inverse).astype(BF16)))
        hi, lo = split2(jnp.concatenate(weights, axis=0))
        sums = dot_t(hi, values) + dot_t(lo, values)
        out_col = iota((SRC * IPB, width), 1)
        picked = sums[0 : SRC * IPB]
        for h in range(1, width // HEAD):
            picked = jnp.where(
                out_col >= h * HEAD, sums[h * SRC * IPB : (h + 1) * SRC * IPB], picked
            )
        pooled[:, 0:width] += picked

    take_near(0, True)
    send_near(2)
    take_near(1, True)
    send_near(3)
    own_to_far(last).start()

    r = iota((SRC * IPB, 1), 0)
    label = jnp.zeros((SRC * IPB, 1), jnp.int32)
    place = jnp.zeros((SRC * IPB, 1), jnp.int32)
    count = jnp.ones((SRC * IPB, 1), jnp.int32)
    for k in range(SRC):
        for n in range(IPB):
            here = r == k * IPB + n
            label = jnp.where(here, info_ref[SRC + k, n], label)
            place = jnp.where(here, info_ref[0, IPB + k] * IPB + n, place)
            count = jnp.where(here, info_ref[k, n], count)
    inverse_count[...] = jnp.broadcast_to(1.0 / count.astype(F32), inverse_count.shape)
    col = iota((SRC * IPB, 256), 1)
    marks[...] = jnp.zeros_like(marks)
    for at, value in ((LABEL_HI, label // 8), (LABEL_LO, label % 8), (PLACE, place)):
        marks[...] = jnp.where(col == at, value.astype(F32), marks[...])

    def image_rows():
        means = (pooled[...] * inverse_count[...]).astype(BF16).astype(F32)
        squares = jnp.sum(means * means, axis=1, keepdims=True)
        sq0 = squares.astype(BF16).astype(F32)
        sq1 = (squares - sq0).astype(BF16).astype(F32)
        extended = jnp.where(col == SQ0, sq0, 0.0)
        extended = jnp.where(col == SQ1, sq1, extended)
        return jnp.where(
            col < width, means, jnp.where(col == SQ2, squares - sq0 - sq1, extended)
        )

    def embed_copy(d):
        return remote(
            pack_rows.at[p], pack_rows.at[p], e_send.at[d], e_recv.at[p], {"pack": (p + d) % n_pack}
        )

    def slot(s, carry):
        @pl.when(s == 1)
        def _():
            take_near(2, True)

        @pl.when(s == 2)
        def _():
            take_near(last, False)

        @pl.when(s < last)
        def _():
            got(s, 6, rows.at[s, far, pl.ds(0, mid)]).wait_recv()
            got(s, 8, rows.at[s, far, pl.ds(mid, mid)]).wait_recv()

        @pl.when(s == last)
        def _():
            got(s, 3, rows.at[s, far]).wait_recv()

        share(s, far, 7).start()

        @pl.when(s == last)
        def _():
            pack_rows[p] = (image_rows() + marks[...]).astype(BF16)
            for d in far_first(n_pack):
                embed_copy(d).start()

        for k, whose in ((2, chip), (4, left // 2), (5, right // 2)):
            got(s, k, rows.at[s, whose * 2 + 1 - core]).wait_recv()
        near = project(s, (chip, left // 2, right // 2))
        got(s, 7, rows.at[s, far + 1 - 2 * core]).wait_recv()
        attend(s, near + project(s, (far // 2,)))
        return carry

    lax.fori_loop(0, SRC, slot, 0)

    whole = image_rows()
    late_rows[p, 0:IPB, :] = whole[last * IPB :, 0:128]
    late_rows[p, IPB : 2 * IPB, :] = whole[last * IPB :, 128:256]

    def late_copy(d):
        return remote(
            late_rows.at[p], late_rows.at[p], l_send.at[d], l_recv.at[p], {"pack": (p + d) % n_pack}
        )

    for d in far_first(n_pack):
        late_copy(d).start()

    for d in range(1, n_dp):
        src = (g + d) % n_dp
        remote(
            text_rows.at[src], text_rows.at[src], t_send.at[d], t_recv.at[src], {"dp": src}
        ).wait_recv()
    n_texts = n_dp * text_rows.shape[1]
    text_all = text_rows[...].reshape(n_texts, 256)
    text_all = jnp.where(iota((n_texts, 256), 1) < width, text_all, 0.0)
    text_squares = jnp.sum(text_all * text_all, axis=1, keepdims=True)
    text_bf = text_all.astype(BF16)
    pick = iota((16, 256), 1)
    is_square = (pick >= SQ0) & (pick <= SQ2)
    low = iota((16, 256), 0) < 8
    reads = jnp.where(low & is_square, 1.0, 0.0)
    reads = jnp.where(jnp.logical_not(low) & (pick == LABEL_HI), 8.0, reads)
    reads = jnp.where(jnp.logical_not(low) & (pick == LABEL_LO), 1.0, reads)
    left_side = jnp.concatenate([text_bf, reads.astype(BF16)], axis=0)

    for d in range(1, n_pack):
        src = (p + d) % n_pack
        remote(
            pack_rows.at[src], pack_rows.at[src], e_send.at[d], e_recv.at[src], {"pack": src}
        ).wait_recv()

    n_slots = n_pack * SRC * IPB
    n_images = n_pack * DEST * IPB
    loose = pack_rows[...].reshape(n_slots, 256)
    find = jnp.where(iota((128, 256), 1) == PLACE, 1.0, 0.0).astype(BF16)
    placing = dot_t(find, loose) == iota((128, n_slots), 0).astype(F32)
    placing = jnp.where(placing, 1.0, 0.0).astype(BF16)
    early = dot(placing, loose)
    slot_row = iota((n_slots, n_pack * 8), 0)
    late_row = iota((n_slots, n_pack * 8), 1)
    pair = (slot_row // 16 == late_row // 8) & (slot_row % 16 >= last * IPB)
    pair = pair & (slot_row % IPB == late_row % IPB)
    first = late_row % 8 < IPB
    first_placing = dot(placing, jnp.where(pair & first, 1.0, 0.0).astype(BF16)).astype(BF16)
    second_placing = dot(placing, jnp.where(pair & jnp.logical_not(first), 1.0, 0.0).astype(BF16))
    second_placing = second_placing.astype(BF16)

    for d in range(1, n_pack):
        src = (p + d) % n_pack
        remote(
            late_rows.at[src], late_rows.at[src], l_send.at[d], l_recv.at[src], {"pack": src}
        ).wait_recv()
    late = late_rows[...].reshape(n_pack * 8, 128).astype(BF16)
    late = jnp.concatenate([dot(first_placing, late), dot(second_placing, late)], axis=1)
    packed = (early + late).astype(BF16)

    products = dot_t(left_side, packed)
    image_lane = iota((n_texts, 128), 1)
    sims[m, 0:n_texts, :] = jnp.where(image_lane < n_images, products[0:n_texts], text_squares)
    sims[m, n_texts : n_texts + 8, :] = products[n_texts : n_texts + 8]
    labels = products[n_texts + 8 : n_texts + 9]

    def sims_copy(k):
        to = (far, right, left)[k]
        return remote(sims.at[m], sims.at[m], s_send.at[k], s_recv.at[k], {"mp": to})

    for k in range(3):
        sims_copy(k).start()
    text_row = iota((n_texts, 128), 0)
    matching = labels == (((text_row // 8) * n_pack + p) * 8 + text_row % 8).astype(F32)
    sign = jnp.where(matching, 1.0, -1.0)
    for k, src in enumerate((far, left, right)):
        remote(sims.at[src], sims.at[src], s_send.at[k], s_recv.at[k], {"mp": src}).wait_recv()
    halves[core] = (sims[core] + sims[2 + core]) + (sims[4 + core] + sims[6 + core])
    half_copy = remote(
        halves.at[core], halves.at[core], s_send.at[3], s_recv.at[3], {"mp": twin}
    )
    half_copy.start()
    half_copy.wait_recv()
    total = halves[0] + halves[1]
    cosine = total[0:n_texts]
    image_scale = lax.rsqrt(total[n_texts : n_texts + 1] + 1e-06)
    text_scale = lax.rsqrt(
        jnp.sum(jnp.where(image_lane == n_images, cosine, 0.0), axis=1, keepdims=True) + 1e-06
    )
    heat = heat_ref[0]
    logits = heat * cosine * image_scale * text_scale + shift_ref[0]
    slopes = -sign * jax.nn.sigmoid(-sign * logits) * heat
    slopes = jnp.where(image_lane < n_images, slopes, 0.0)

    hi, lo = split2(slopes * text_scale)
    contract0 = (((0,), (0,)), ((), ()))
    image_part = lax.dot_general(hi, text_bf, contract0, preferred_element_type=F32)
    image_part += lax.dot_general(lo, text_bf, contract0, preferred_element_type=F32)
    own_image[...] = image_part[0:n_images].reshape(n_pack, 8, 256)

    def image_copy(d):
        to = (p + d) % n_pack
        return remote(
            own_image.at[to], image_terms.at[p], iz_send.at[d], iz_recv.at[p], {"pack": to}
        )

    for d in far_first(n_pack):
        image_copy(d).start()

    hi, lo = split2(slopes * jnp.where(iota((1, 128), 1) < n_images, image_scale, 0.0))
    text_part = dot(hi, packed) + dot(lo, packed)
    own_text[...] = text_part.reshape(n_dp, 8, 256)

    def text_term_copy(d):
        to = (g + d) % n_dp
        return remote(own_text.at[to], text_terms.at[g], ty_send.at[d], ty_recv.at[g], {"dp": to})

    for d in far_first(n_dp):
        text_term_copy(d).start()

    image_terms[p] = own_image[p]
    text_terms[g] = own_text[g]
    for d in range(1, n_dp):
        src = (g + d) % n_dp
        remote(
            own_text.at[src], text_terms.at[src], ty_send.at[d], ty_recv.at[src], {"dp": src}
        ).wait_recv()
    out[1] = jnp.sum(text_terms[...], axis=0)[:, 0:width]
    for d in range(1, n_pack):
        src = (p + d) % n_pack
        remote(
            own_image.at[src], image_terms.at[src], iz_send.at[d], iz_recv.at[src], {"pack": src}
        ).wait_recv()
    out[0] = jnp.sum(image_terms[...], axis=0)[:, 0:width]

    for s in range(SRC):
        own_to_right(s).wait_send()
        own_to_left(s).wait_send()
        own_to_twin(s).wait_send()
        share(s, left, 4).wait_send()
        share(s, right, 5).wait_send()
        share(s, far, 7).wait_send()
        if s < last:
            pass_right(s).wait_send()
            pass_left(s).wait_send()
        else:
            own_to_far(s).wait_send()
    for d in range(1, n_dp):
        text_copy(d).wait_send()
        text_term_copy(d).wait_send()
    for d in range(1, n_pack):
        embed_copy(d).wait_send()
        late_copy(d).wait_send()
        image_copy(d).wait_send()
    for k in range(3):
        sims_copy(k).wait_send()
    half_copy.wait_send()


def on_device(
    n_dp,
    n_pack,
    n_mp,
    tile_activity,
    tokens_per_picture,
    slot_destinations,
    caption_indices,
    attention_projections,
    caption_vectors,
    score_inverse_heat,
    score_shift,
):
    width = caption_vectors.shape[1]
    depth = attention_projections.shape[1]
    n_texts = n_dp * caption_vectors.shape[0]
    block_info = jnp.pad(tokens_per_picture, ((0, SRC), (0, 128 - IPB)))
    block_info += jnp.pad(caption_indices, ((SRC, 0), (0, 128 - IPB)))
    block_info += jnp.pad(slot_destinations[None, :], ((0, 2 * SRC - 1), (IPB, 128 - IPB - SRC)))
    vmem = pl.BlockSpec(memory_space=pltpu.VMEM)
    hbm = pl.BlockSpec(memory_space=pltpu.HBM)
    dma = pltpu.SemaphoreType.DMA
    grads = pl.pallas_call(
        functools.partial(kernel, n_dp, n_pack, n_mp),
        out_shape=jax.ShapeDtypeStruct((2, *caption_vectors.shape), F32),
        in_specs=[hbm, hbm, hbm, vmem, hbm, hbm],
        out_specs=vmem,
        scratch_shapes=[
            pltpu.SMEM(block_info.shape, jnp.int32),
            pltpu.SMEM((1,), F32),
            pltpu.SMEM((1,), F32),
            pltpu.VMEM((3, width, depth), BF16),
            pltpu.VMEM((SRC, n_mp, width, BLK), BF16),
            pltpu.VMEM((SRC * IPB, 256), F32),
            pltpu.VMEM((n_dp, 8, 256), F32),
            pltpu.VMEM((n_pack, SRC * IPB, 256), BF16),
            pltpu.VMEM((n_pack, 8, 128), F32),
            pltpu.VMEM((SRC * IPB, 256), F32),
            pltpu.VMEM((SRC * IPB, 256), F32),
            pltpu.VMEM((n_mp, n_texts + 8, 128), F32),
            pltpu.VMEM((2, n_texts + 8, 128), F32),
            pltpu.VMEM((n_dp, 8, 256), F32),
            pltpu.VMEM((n_pack, 8, 256), F32),
            pltpu.VMEM((n_dp, 8, 256), F32),
            pltpu.VMEM((n_pack, 8, 256), F32),
            dma((5,)),
            dma((SRC, 9)),
            dma((SRC, 9)),
            dma((n_dp,)),
            dma((n_dp,)),
            dma((n_pack,)),
            dma((n_pack,)),
            dma((n_pack,)),
            dma((n_pack,)),
            dma((4,)),
            dma((4,)),
            dma((n_dp,)),
            dma((n_dp,)),
            dma((n_pack,)),
            dma((n_pack,)),
        ],
        compiler_params=pltpu.CompilerParams(
            collective_id=0, has_side_effects=True, vmem_limit_bytes=55040 * 1024
        ),
        name="contrastive_step",
    )(
        jnp.swapaxes(tile_activity, 1, 2),
        block_info,
        jnp.swapaxes(attention_projections, 1, 2),
        caption_vectors,
        score_inverse_heat,
        score_shift,
    )
    return grads[0], grads[1]


def solution(mesh):
    sizes = (mesh.shape["dp"], mesh.shape["pack"], mesh.shape["mp"])
    return jax.shard_map(
        functools.partial(on_device, *sizes),
        mesh=mesh,
        in_specs=(
            P(("dp", "pack"), None, "mp"),
            P(("dp", "pack"), None),
            P(("dp", "pack")),
            P(("dp", "pack"), None),
            P(None, None, "mp"),
            P(("dp", "pack"), "mp"),
            P(),
            P(),
        ),
        out_specs=(P(("dp", "pack"), "mp"), P(("dp", "pack"), "mp")),
        check_vma=False,
    )
```

```python
import functools

import jax
import jax.numpy as jnp
from jax import lax
from jax.experimental import pallas as pl
from jax.experimental.pallas import tpu as pltpu
from jax.sharding import PartitionSpec as P

HEAD = 64
BLK = 256
IPB = 4
DEST = 2
SRC = 4
F32 = jnp.float32
BF16 = jnp.bfloat16
MESH = pl.DeviceIdType.MESH

LABEL_HI, LABEL_LO, PLACE, SQ0, SQ1, SQ2 = 192, 193, 194, 195, 196, 197


def dot(a, b):
    return jnp.dot(a, b, preferred_element_type=F32)


def dot_t(a, b):
    return lax.dot_general(a, b, (((1,), (1,)), ((), ())), preferred_element_type=F32)


def iota(shape, axis):
    return lax.broadcasted_iota(jnp.int32, shape, axis)


def split2(a):
    hi = a.astype(BF16)
    return hi, (a - hi.astype(F32)).astype(BF16)


def far_first(n):
    return sorted(range(1, n), key=lambda d: -min(d, n - d))


def kernel(
    n_dp,
    n_pack,
    n_mp,
    tile_hbm,
    info_hbm,
    proj_hbm,
    texts_ref,
    heat_hbm,
    shift_hbm,
    out,
    info_ref,
    heat_ref,
    shift_ref,
    proj,
    rows,
    pooled,
    text_rows,
    pack_rows,
    late_rows,
    marks,
    inverse_count,
    sims,
    halves,
    own_text,
    own_image,
    text_terms,
    image_terms,
    load_sem,
    x_send,
    x_recv,
    t_send,
    t_recv,
    e_send,
    e_recv,
    l_send,
    l_recv,
    s_send,
    s_recv,
    ty_send,
    ty_recv,
    iz_send,
    iz_recv,
):
    g, p, m = lax.axis_index("dp"), lax.axis_index("pack"), lax.axis_index("mp")
    chips = n_mp // 2
    chip, core = m // 2, m % 2
    right = ((chip + 1) % chips) * 2 + core
    left = ((chip + chips - 1) % chips) * 2 + core
    far = ((chip + 2) % chips) * 2 + core
    twin = chip * 2 + 1 - core
    width = texts_ref.shape[1]

    load_tile = pltpu.make_async_copy(tile_hbm, rows.at[:, m], load_sem.at[0])
    load_proj = pltpu.make_async_copy(proj_hbm, proj, load_sem.at[1])
    load_tile.start()
    load_proj.start()
    scalars = [
        pltpu.make_async_copy(src, dst, load_sem.at[2 + i])
        for i, (src, dst) in enumerate(
            (
                (info_hbm, info_ref),
                (heat_hbm, heat_ref),
                (shift_hbm, shift_ref),
            )
        )
    ]
    for copy in scalars:
        copy.start()

    barrier = pltpu.get_barrier_semaphore()
    for d in range(1, n_mp):
        pl.semaphore_signal(barrier, inc=1, device_id={"mp": (m + d) % n_mp}, device_id_type=MESH)
    for d in range(1, n_dp):
        pl.semaphore_signal(barrier, inc=1, device_id={"dp": (g + d) % n_dp}, device_id_type=MESH)
    for d in range(1, n_pack):
        pl.semaphore_signal(
            barrier, inc=1, device_id={"pack": (p + d) % n_pack}, device_id_type=MESH
        )

    text_rows[g] = jnp.zeros((8, 256), F32)
    text_rows[g, :, 0:width] = texts_ref[...].astype(F32)

    pl.semaphore_wait(barrier, n_mp + n_dp + n_pack - 3)

    def remote(src, dst, send, recv, where):
        return pltpu.make_async_remote_copy(
            src_ref=src,
            dst_ref=dst,
            send_sem=send,
            recv_sem=recv,
            device_id=where,
            device_id_type=MESH,
        )

    def own_to_right(s):
        return remote(tile_hbm.at[s], rows.at[s, m], x_send.at[s, 0], x_recv.at[s, 0], {"mp": right})

    def own_to_left(s):
        return remote(tile_hbm.at[s], rows.at[s, m], x_send.at[s, 1], x_recv.at[s, 1], {"mp": left})

    def own_to_twin(s):
        return remote(tile_hbm.at[s], rows.at[s, m], x_send.at[s, 2], x_recv.at[s, 2], {"mp": twin})

    def own_to_far(s):
        return remote(tile_hbm.at[s], rows.at[s, m], x_send.at[s, 3], x_recv.at[s, 3], {"mp": far})

    mid = width // 2

    def pass_right(s):
        part = rows.at[s, left, pl.ds(0, mid)]
        return remote(part, part, x_send.at[s, 6], x_recv.at[s, 6], {"mp": right})

    def pass_left(s):
        part = rows.at[s, right, pl.ds(mid, mid)]
        return remote(part, part, x_send.at[s, 8], x_recv.at[s, 8], {"mp": left})

    def share(s, whose, k):
        part = rows.at[s, whose]
        return remote(part, part, x_send.at[s, k], x_recv.at[s, k], {"mp": twin})

    def got(s, k, part):
        return remote(part, part, x_send.at[s, k], x_recv.at[s, k], {"mp": twin})

    def send_near(s):
        own_to_right(s).start()
        own_to_left(s).start()
        own_to_twin(s).start()

    def take_near(s, hand_on):
        got(s, 0, rows.at[s, left]).wait_recv()
        if hand_on:
            pass_right(s).start()
        share(s, left, 4).start()
        got(s, 1, rows.at[s, right]).wait_recv()
        if hand_on:
            pass_left(s).start()
        share(s, right, 5).start()

    last = SRC - 1
    send_near(0)
    send_near(1)

    def text_copy(d):
        return remote(
            text_rows.at[g], text_rows.at[g], t_send.at[d], t_recv.at[g], {"dp": (g + d) % n_dp}
        )

    for d in far_first(n_dp):
        text_copy(d).start()

    load_proj.wait()
    load_tile.wait()
    for copy in scalars:
        copy.wait()
    pooled[...] = jnp.zeros_like(pooled)

    def project(s, whose):
        weights = [
            proj[:, :, pl.ds(pl.multiple_of(c * 2 * width, 128), 2 * width)] for c in whose
        ]
        features = [rows[s, pl.ds(c * 2, 2)].reshape(2 * width, BLK) for c in whose]
        return dot(
            jnp.concatenate(weights, axis=2).reshape(3 * width, len(whose) * 2 * width),
            jnp.concatenate(features, axis=0),
        )

    def attend(s, projected):
        e1 = info_ref[s, 0]
        e2 = e1 + info_ref[s, 1]
        e3 = e2 + info_ref[s, 2]

        def image_of(position):
            return (
                (position >= e1).astype(jnp.int32)
                + (position >= e2).astype(jnp.int32)
                + (position >= e3).astype(jnp.int32)
            )

        image = iota((16, BLK), 0)
        same = image_of(iota((16, BLK), 1)) == image
        query_extra = jnp.where((image < IPB) & same, -1e30, 0.0).astype(BF16)
        key_extra = jnp.where((image < IPB) & jnp.logical_not(same), 1.0, 0.0).astype(BF16)

        queries = (projected[0:width] * HEAD**-0.5).astype(BF16)
        keys = projected[width : 2 * width].astype(BF16)
        values = projected[2 * width : 3 * width].astype(BF16)

        row16 = iota((SRC * IPB, BLK), 0)
        member = (row16 // IPB == s) & (row16 % IPB == image_of(iota((SRC * IPB, BLK), 1)))
        member = jnp.where(member, 1.0, 0.0).astype(BF16)
        weights = []
        for h in range(width // HEAD):
            head = slice(h * HEAD, (h + 1) * HEAD)
            scores = lax.dot_general(
                jnp.concatenate([keys[head], key_extra], axis=0),
                jnp.concatenate([queries[head], query_extra], axis=0),
                (((0,), (0,)), ((), ())),
                preferred_element_type=F32,
            )
            exponent = jnp.exp(scores - jnp.max(scores, axis=0, keepdims=True))
            inverse = 1.0 / jnp.sum(exponent, axis=0, keepdims=True)
            weights.append(dot_t(member, (exponent * inverse).astype(BF16)))
        hi, lo = split2(jnp.concatenate(weights, axis=0))
        sums = dot_t(hi, values) + dot_t(lo, values)
        out_col = iota((SRC * IPB, width), 1)
        picked = sums[0 : SRC * IPB]
        for h in range(1, width // HEAD):
            picked = jnp.where(
                out_col >= h * HEAD, sums[h * SRC * IPB : (h + 1) * SRC * IPB], picked
            )
        pooled[:, 0:width] += picked

    take_near(0, True)
    send_near(2)
    take_near(1, True)
    send_near(3)
    own_to_far(last).start()

    r = iota((SRC * IPB, 1), 0)
    label = jnp.zeros((SRC * IPB, 1), jnp.int32)
    place = jnp.zeros((SRC * IPB, 1), jnp.int32)
    count = jnp.ones((SRC * IPB, 1), jnp.int32)
    for k in range(SRC):
        for n in range(IPB):
            here = r == k * IPB + n
            label = jnp.where(here, info_ref[SRC + k, n], label)
            place = jnp.where(here, info_ref[0, IPB + k] * IPB + n, place)
            count = jnp.where(here, info_ref[k, n], count)
    inverse_count[...] = jnp.broadcast_to(1.0 / count.astype(F32), inverse_count.shape)
    col = iota((SRC * IPB, 256), 1)
    marks[...] = jnp.zeros_like(marks)
    for at, value in ((LABEL_HI, label // 8), (LABEL_LO, label % 8), (PLACE, place)):
        marks[...] = jnp.where(col == at, value.astype(F32), marks[...])

    def image_rows():
        means = (pooled[...] * inverse_count[...]).astype(BF16).astype(F32)
        squares = jnp.sum(means * means, axis=1, keepdims=True)
        sq0 = squares.astype(BF16).astype(F32)
        sq1 = (squares - sq0).astype(BF16).astype(F32)
        extended = jnp.where(col == SQ0, sq0, 0.0)
        extended = jnp.where(col == SQ1, sq1, extended)
        return jnp.where(
            col < width, means, jnp.where(col == SQ2, squares - sq0 - sq1, extended)
        )

    def embed_copy(d):
        return remote(
            pack_rows.at[p], pack_rows.at[p], e_send.at[d], e_recv.at[p], {"pack": (p + d) % n_pack}
        )

    def slot(s, carry):
        @pl.when(s == 1)
        def _():
            take_near(2, True)

        @pl.when(s == 2)
        def _():
            take_near(last, False)

        @pl.when(s < last)
        def _():
            got(s, 6, rows.at[s, far, pl.ds(0, mid)]).wait_recv()
            got(s, 8, rows.at[s, far, pl.ds(mid, mid)]).wait_recv()

        @pl.when(s == last)
        def _():
            got(s, 3, rows.at[s, far]).wait_recv()

        share(s, far, 7).start()

        @pl.when(s == last)
        def _():
            pack_rows[p] = (image_rows() + marks[...]).astype(BF16)
            for d in far_first(n_pack):
                embed_copy(d).start()

        for k, whose in ((2, chip), (4, left // 2), (5, right // 2)):
            got(s, k, rows.at[s, whose * 2 + 1 - core]).wait_recv()
        near = project(s, (chip, left // 2, right // 2))
        got(s, 7, rows.at[s, far + 1 - 2 * core]).wait_recv()
        attend(s, near + project(s, (far // 2,)))
        return carry

    lax.fori_loop(0, SRC, slot, 0)

    whole = image_rows()
    late_rows[p, 0:IPB, :] = whole[last * IPB :, 0:128]
    late_rows[p, IPB : 2 * IPB, :] = whole[last * IPB :, 128:256]

    def late_copy(d):
        return remote(
            late_rows.at[p], late_rows.at[p], l_send.at[d], l_recv.at[p], {"pack": (p + d) % n_pack}
        )

    for d in far_first(n_pack):
        late_copy(d).start()

    for d in range(1, n_dp):
        src = (g + d) % n_dp
        remote(
            text_rows.at[src], text_rows.at[src], t_send.at[d], t_recv.at[src], {"dp": src}
        ).wait_recv()
    n_texts = n_dp * text_rows.shape[1]
    text_all = text_rows[...].reshape(n_texts, 256)
    text_all = jnp.where(iota((n_texts, 256), 1) < width, text_all, 0.0)
    text_squares = jnp.sum(text_all * text_all, axis=1, keepdims=True)
    text_bf = text_all.astype(BF16)
    pick = iota((16, 256), 1)
    is_square = (pick >= SQ0) & (pick <= SQ2)
    low = iota((16, 256), 0) < 8
    reads = jnp.where(low & is_square, 1.0, 0.0)
    reads = jnp.where(jnp.logical_not(low) & (pick == LABEL_HI), 8.0, reads)
    reads = jnp.where(jnp.logical_not(low) & (pick == LABEL_LO), 1.0, reads)
    left_side = jnp.concatenate([text_bf, reads.astype(BF16)], axis=0)

    for d in range(1, n_pack):
        src = (p + d) % n_pack
        remote(
            pack_rows.at[src], pack_rows.at[src], e_send.at[d], e_recv.at[src], {"pack": src}
        ).wait_recv()

    n_slots = n_pack * SRC * IPB
    n_images = n_pack * DEST * IPB
    loose = pack_rows[...].reshape(n_slots, 256)
    find = jnp.where(iota((128, 256), 1) == PLACE, 1.0, 0.0).astype(BF16)
    placing = dot_t(find, loose) == iota((128, n_slots), 0).astype(F32)
    placing = jnp.where(placing, 1.0, 0.0).astype(BF16)
    early = dot(placing, loose)
    slot_row = iota((n_slots, n_pack * 8), 0)
    late_row = iota((n_slots, n_pack * 8), 1)
    pair = (slot_row // 16 == late_row // 8) & (slot_row % 16 >= last * IPB)
    pair = pair & (slot_row % IPB == late_row % IPB)
    first = late_row % 8 < IPB
    first_placing = dot(placing, jnp.where(pair & first, 1.0, 0.0).astype(BF16)).astype(BF16)
    second_placing = dot(placing, jnp.where(pair & jnp.logical_not(first), 1.0, 0.0).astype(BF16))
    second_placing = second_placing.astype(BF16)

    for d in range(1, n_pack):
        src = (p + d) % n_pack
        remote(
            late_rows.at[src], late_rows.at[src], l_send.at[d], l_recv.at[src], {"pack": src}
        ).wait_recv()
    late = late_rows[...].reshape(n_pack * 8, 128).astype(BF16)
    late = jnp.concatenate([dot(first_placing, late), dot(second_placing, late)], axis=1)
    packed = (early + late).astype(BF16)

    products = dot_t(left_side, packed)
    image_lane = iota((n_texts, 128), 1)
    sims[m, 0:n_texts, :] = jnp.where(image_lane < n_images, products[0:n_texts], text_squares)
    sims[m, n_texts : n_texts + 8, :] = products[n_texts : n_texts + 8]
    labels = products[n_texts + 8 : n_texts + 9]

    def sims_copy(k):
        to = (far, right, left)[k]
        return remote(sims.at[m], sims.at[m], s_send.at[k], s_recv.at[k], {"mp": to})

    for k in range(3):
        sims_copy(k).start()
    text_row = iota((n_texts, 128), 0)
    matching = labels == (((text_row // 8) * n_pack + p) * 8 + text_row % 8).astype(F32)
    sign = jnp.where(matching, 1.0, -1.0)
    for k, src in enumerate((far, left, right)):
        remote(sims.at[src], sims.at[src], s_send.at[k], s_recv.at[k], {"mp": src}).wait_recv()
    halves[core] = (sims[core] + sims[2 + core]) + (sims[4 + core] + sims[6 + core])
    half_copy = remote(
        halves.at[core], halves.at[core], s_send.at[3], s_recv.at[3], {"mp": twin}
    )
    half_copy.start()
    half_copy.wait_recv()
    total = halves[0] + halves[1]
    cosine = total[0:n_texts]
    image_scale = lax.rsqrt(total[n_texts : n_texts + 1] + 1e-06)
    text_scale = lax.rsqrt(
        jnp.sum(jnp.where(image_lane == n_images, cosine, 0.0), axis=1, keepdims=True) + 1e-06
    )
    heat = heat_ref[0]
    logits = heat * cosine * image_scale * text_scale + shift_ref[0]
    slopes = -sign * jax.nn.sigmoid(-sign * logits) * heat
    slopes = jnp.where(image_lane < n_images, slopes, 0.0)

    hi, lo = split2(slopes * text_scale)
    contract0 = (((0,), (0,)), ((), ()))
    image_part = lax.dot_general(hi, text_bf, contract0, preferred_element_type=F32)
    image_part += lax.dot_general(lo, text_bf, contract0, preferred_element_type=F32)
    for to in range(n_pack):
        part = image_part[to * 8 : to * 8 + 8]
        own_image[to, 0] = part[0:4, 0:128]
        own_image[to, 1] = part[4:8, 0:128]
        own_image[to, 2] = jnp.concatenate([part[0:4, 128:192], part[4:8, 128:192]], axis=1)

    def image_copy(d):
        to = (p + d) % n_pack
        return remote(
            own_image.at[to], image_terms.at[p], iz_send.at[d], iz_recv.at[p], {"pack": to}
        )

    for d in far_first(n_pack):
        image_copy(d).start()

    hi, lo = split2(slopes * jnp.where(iota((1, 128), 1) < n_images, image_scale, 0.0))
    text_part = dot(hi, packed) + dot(lo, packed)
    own_text[...] = text_part.reshape(n_dp, 8, 256)

    def text_term_copy(d):
        to = (g + d) % n_dp
        return remote(own_text.at[to], text_terms.at[g], ty_send.at[d], ty_recv.at[g], {"dp": to})

    for d in far_first(n_dp):
        text_term_copy(d).start()

    image_terms[p] = own_image[p]
    text_terms[g] = own_text[g]
    for d in range(1, n_dp):
        src = (g + d) % n_dp
        remote(
            own_text.at[src], text_terms.at[src], ty_send.at[d], ty_recv.at[src], {"dp": src}
        ).wait_recv()
    out[1] = jnp.sum(text_terms[...], axis=0)[:, 0:width]
    for d in range(1, n_pack):
        src = (p + d) % n_pack
        remote(
            own_image.at[src], image_terms.at[src], iz_send.at[d], iz_recv.at[src], {"pack": src}
        ).wait_recv()
    pieces = jnp.sum(image_terms[...], axis=0)
    out[0, 0:4, 0:128] = pieces[0]
    out[0, 4:8, 0:128] = pieces[1]
    out[0, 0:4, 128:192] = pieces[2, :, 0:64]
    out[0, 4:8, 128:192] = pieces[2, :, 64:128]

    for s in range(SRC):
        own_to_right(s).wait_send()
        own_to_left(s).wait_send()
        own_to_twin(s).wait_send()
        share(s, left, 4).wait_send()
        share(s, right, 5).wait_send()
        share(s, far, 7).wait_send()
        if s < last:
            pass_right(s).wait_send()
            pass_left(s).wait_send()
        else:
            own_to_far(s).wait_send()
    for d in range(1, n_dp):
        text_copy(d).wait_send()
        text_term_copy(d).wait_send()
    for d in range(1, n_pack):
        embed_copy(d).wait_send()
        late_copy(d).wait_send()
        image_copy(d).wait_send()
    for k in range(3):
        sims_copy(k).wait_send()
    half_copy.wait_send()


def on_device(
    n_dp,
    n_pack,
    n_mp,
    tile_activity,
    tokens_per_picture,
    slot_destinations,
    caption_indices,
    attention_projections,
    caption_vectors,
    score_inverse_heat,
    score_shift,
):
    width = caption_vectors.shape[1]
    depth = attention_projections.shape[1]
    n_texts = n_dp * caption_vectors.shape[0]
    block_info = jnp.pad(tokens_per_picture, ((0, SRC), (0, 128 - IPB)))
    block_info += jnp.pad(caption_indices, ((SRC, 0), (0, 128 - IPB)))
    block_info += jnp.pad(slot_destinations[None, :], ((0, 2 * SRC - 1), (IPB, 128 - IPB - SRC)))
    vmem = pl.BlockSpec(memory_space=pltpu.VMEM)
    hbm = pl.BlockSpec(memory_space=pltpu.HBM)
    dma = pltpu.SemaphoreType.DMA
    grads = pl.pallas_call(
        functools.partial(kernel, n_dp, n_pack, n_mp),
        out_shape=jax.ShapeDtypeStruct((2, *caption_vectors.shape), F32),
        in_specs=[hbm, hbm, hbm, vmem, hbm, hbm],
        out_specs=vmem,
        scratch_shapes=[
            pltpu.SMEM(block_info.shape, jnp.int32),
            pltpu.SMEM((1,), F32),
            pltpu.SMEM((1,), F32),
            pltpu.VMEM((3, width, depth), BF16),
            pltpu.VMEM((SRC, n_mp, width, BLK), BF16),
            pltpu.VMEM((SRC * IPB, 256), F32),
            pltpu.VMEM((n_dp, 8, 256), F32),
            pltpu.VMEM((n_pack, SRC * IPB, 256), BF16),
            pltpu.VMEM((n_pack, 8, 128), F32),
            pltpu.VMEM((SRC * IPB, 256), F32),
            pltpu.VMEM((SRC * IPB, 256), F32),
            pltpu.VMEM((n_mp, n_texts + 8, 128), F32),
            pltpu.VMEM((2, n_texts + 8, 128), F32),
            pltpu.VMEM((n_dp, 8, 256), F32),
            pltpu.VMEM((n_pack, 3, 4, 128), F32),
            pltpu.VMEM((n_dp, 8, 256), F32),
            pltpu.VMEM((n_pack, 3, 4, 128), F32),
            dma((5,)),
            dma((SRC, 9)),
            dma((SRC, 9)),
            dma((n_dp,)),
            dma((n_dp,)),
            dma((n_pack,)),
            dma((n_pack,)),
            dma((n_pack,)),
            dma((n_pack,)),
            dma((4,)),
            dma((4,)),
            dma((n_dp,)),
            dma((n_dp,)),
            dma((n_pack,)),
            dma((n_pack,)),
        ],
        compiler_params=pltpu.CompilerParams(
            collective_id=0, has_side_effects=True, vmem_limit_bytes=55040 * 1024
        ),
        name="contrastive_step",
    )(
        jnp.swapaxes(tile_activity, 1, 2),
        block_info,
        jnp.swapaxes(attention_projections, 1, 2),
        caption_vectors,
        score_inverse_heat,
        score_shift,
    )
    return grads[0], grads[1]


def solution(mesh):
    sizes = (mesh.shape["dp"], mesh.shape["pack"], mesh.shape["mp"])
    return jax.shard_map(
        functools.partial(on_device, *sizes),
        mesh=mesh,
        in_specs=(
            P(("dp", "pack"), None, "mp"),
            P(("dp", "pack"), None),
            P(("dp", "pack")),
            P(("dp", "pack"), None),
            P(None, None, "mp"),
            P(("dp", "pack"), "mp"),
            P(),
            P(),
        ),
        out_specs=(P(("dp", "pack"), "mp"), P(("dp", "pack"), "mp")),
        check_vma=False,
    )
```
